32 devices in a mesh: seq: 16 (over z, x, core), chan: 2 (over y).
Axes of the slice: x: 2, y: 2, z: 4, core: 2. Of those that a mesh axis runs over, the one named last changes fastest.
Arguments:
- inputs: bfloat16 [512, 262144], P('chan', 'seq'), may hold values from -6 to 6
- gate_acts: bfloat16 [512, 262144], P('chan', 'seq'), may hold values from -6 to 6
- out_grad: bfloat16 [512, 262144], P('chan', 'seq'), may hold values from -6 to 6
- first_factor: bfloat16 [512, 512], replicated, may hold values from -0.25 to 0.25
- second_factor: bfloat16 [512, 512], replicated, may hold values from -0.25 to 0.25
Outputs:
- input_grad: bfloat16 [512, 262144], P('chan', 'seq')
- gate_grad: bfloat16 [512, 262144], P('chan', 'seq')
- first_grad: float32 [512, 512], P('seq')
- second_grad: float32 [512, 512], P('seq')
The draws below stay inside these ranges and needn't reach their ends.
All inputs are finite; a program needn't handle non-finite values.
Results may differ from the reference program's by a relative error of at most 0.0057.
Values may be sent and summed in bfloat16 or wider, within the bound.
A program may use at most 192 MiB of HBM per device.

```python
import math
import jax
import jax.numpy as jnp
from jax import lax

N1 = 512
N2 = 512
CHANNELS = 512
LENGTH = 262144


def steps_of(rng, shape, cuts, least, largest):
    def one(axis_at, parts):
        draws = jax.random.uniform(jax.random.fold_in(jax.random.fold_in(rng, 6), axis_at), (parts,), jnp.float32, least / len(cuts), largest / len(cuts))
        return jnp.repeat(jnp.exp(draws), shape[axis_at] // parts).reshape((-1,) + (1,) * (len(shape) - axis_at - 1))

    level = one(*cuts[0])
    for cut in cuts[1:]:
        level = level * one(*cut)
    return level


def gaussian(rng, dims, deviation, bound, shards=(), held_as=jnp.bfloat16):
    gain = steps_of(rng, dims, shards, -0.22, 0.18) if shards else 1.0
    values = jax.random.normal(rng, dims, jnp.float32) * deviation * gain
    return jnp.minimum(jnp.maximum(values, -bound), bound).astype(held_as)


def setup_inputs(seed: int = 0) -> dict:
    keys = jax.random.split(jax.random.key(seed), 6)
    inputs = gaussian(keys[0], (CHANNELS, LENGTH), 1.0, 6.0, ((0, 2), (1, 16)))
    gate_acts = gaussian(keys[1], (CHANNELS, LENGTH), 1.0, 6.0, ((0, 2), (1, 16)))
    out_grad = gaussian(keys[2], (CHANNELS, LENGTH), 1.0, 6.0, ((0, 2), (1, 16)))
    first_factor = gaussian(keys[3], (N2, N2), N2 ** -0.5, 0.25)
    second_factor = gaussian(keys[4], (N1, N1), N1 ** -0.5, 0.25)
    return {"inputs": inputs, "gate_acts": gate_acts, "out_grad": out_grad, "first_factor": first_factor, "second_factor": second_factor}


def reference(inputs, gate_acts, out_grad, first_factor, second_factor):
    highest = lax.Precision.HIGHEST
    block_extent = math.gcd(CHANNELS, 32)
    count = CHANNELS // block_extent
    first_mat = first_factor.astype(jnp.float32)
    second_mat = second_factor.astype(jnp.float32)

    def round_keep(value):
        return lax.optimization_barrier(value.astype(jnp.bfloat16)).astype(jnp.float32)

    def step(carry, pieces):
        first_acc, second_acc = carry
        input_block, gate_block, grad_block = pieces
        grid_vals = input_block.astype(jnp.float32).reshape(block_extent, N1, N2)
        inner = round_keep(jnp.einsum('cij,kj->cik', grid_vals, first_mat, precision=highest))
        mixed_out = jnp.einsum('cik,mi->ckm', inner, second_mat, precision=highest)
        gate_vals = gate_block.astype(jnp.float32).reshape(block_extent, N2, N1)
        gradient_entries = grad_block.astype(jnp.float32).reshape(block_extent, N2, N1)
        gate_grad = (gradient_entries * mixed_out).astype(jnp.bfloat16).reshape(block_extent, N1 * N2)
        mixer_gradient = round_keep(gradient_entries * gate_vals)
        inner_grad = round_keep(jnp.einsum('ckm,mi->cik', mixer_gradient, second_mat, precision=highest))
        input_grad = jnp.einsum('cik,kj->cij', inner_grad, first_mat, precision=highest)
        input_grad = input_grad.astype(jnp.bfloat16).reshape(block_extent, N1 * N2)
        second_acc = second_acc + jnp.einsum('ckm,cik->mi', mixer_gradient, inner, precision=highest)
        first_acc = first_acc + jnp.einsum('cik,cij->kj', inner_grad, grid_vals, precision=highest)
        return (first_acc, second_acc), (input_grad, gate_grad)

    stacked = (inputs.reshape(count, block_extent, N1 * N2),
               gate_acts.reshape(count, block_extent, N1 * N2),
               out_grad.reshape(count, block_extent, N1 * N2))
    start = (jnp.zeros((N2, N2), jnp.float32), jnp.zeros((N1, N1), jnp.float32))
    (first_grad, second_grad), (input_grad, gate_grad) = lax.scan(step, start, stacked)
    return (input_grad.reshape(CHANNELS, N1 * N2), gate_grad.reshape(CHANNELS, N1 * N2),
            first_grad, second_grad)
```

```python
import functools

import jax
import jax.numpy as jnp
from jax import lax
from jax.experimental import pallas as pl
from jax.experimental.pallas import tpu as pltpu
from jax.sharding import PartitionSpec as P

BF16 = jnp.bfloat16
F32 = jnp.float32
LANES = 128
PACK = 16
GROUPS = 4


def dot_nn(lhs, rhs):
    return lax.dot_general(lhs, rhs, (((1,), (0,)), ((), ())), preferred_element_type=F32)


def dot_nt(lhs, rhs):
    return lax.dot_general(lhs, rhs, (((1,), (1,)), ((), ())), preferred_element_type=F32)


def dot_tn(lhs, rhs):
    return lax.dot_general(lhs, rhs, (((0,), (0,)), ((), ())), preferred_element_type=F32)


def stream(count, loads, work, store=None):
    def body(step, carry):
        slot = lax.rem(step, 2)

        @pl.when(step + 1 < count)
        def _():
            for load in loads:
                load(step + 1, 1 - slot).start()

        for load in loads:
            load(step, slot).wait()
        if store is not None:

            @pl.when(step >= 2)
            def _():
                store(step - 2, slot).wait()

        work(step, slot)
        if store is not None:
            store(step, slot).start()
        return carry

    for load in loads:
        load(0, 0).start()
    lax.fori_loop(0, count, body, 0)
    if store is not None:
        for step in range(max(count - 2, 0), count):
            store(step, step % 2).wait()


def kernel(
    n, x_hbm, q_hbm, g_hbm, a_ref, bt_ref,
    dx_hbm, dq_hbm, acc1, acc2,
    out1, out2, got1, got2, turned, x_buf, g_buf, q_buf, y_buf,
    x_sem, g_sem, q_sem, y_sem, own_sem, send1, recv1, send2, recv2,
):
    me = lax.axis_index("seq")
    width = x_hbm.shape[0]
    rows, cols = bt_ref.shape[0], a_ref.shape[0]
    row_block, col_block = rows // n, cols // n
    part = row_block // GROUPS

    def hop(d):
        return lax.rem(me + d, n)

    barrier = pltpu.get_barrier_semaphore()

    def greet(d, carry):
        pl.semaphore_signal(
            barrier, inc=1, device_id={"seq": hop(d)}, device_id_type=pl.DeviceIdType.MESH
        )
        return carry

    lax.fori_loop(1, n, greet, 0)

    def load_x(step, slot):
        return pltpu.make_async_copy(
            x_hbm.at[:, pl.ds(pl.multiple_of(step * cols, LANES), cols)],
            x_buf.at[slot], x_sem.at[slot],
        )

    def load_g(step, slot):
        return pltpu.make_async_copy(
            g_hbm.at[:, pl.ds(pl.multiple_of(step * rows, LANES), rows)],
            g_buf.at[slot], g_sem.at[slot],
        )

    def load_q(step, slot):
        return pltpu.make_async_copy(
            q_hbm.at[:, pl.ds(pl.multiple_of(step * rows, LANES), rows)],
            q_buf.at[slot], q_sem.at[slot],
        )

    def send_first(group, peer):
        return pltpu.make_async_remote_copy(
            src_ref=out1.at[
                pl.ds(group * part, part), pl.ds(pl.multiple_of(peer * col_block, PACK), col_block)
            ],
            dst_ref=got1.at[pl.ds(me * row_block + group * part, part)],
            send_sem=send1.at[group], recv_sem=recv1.at[group],
            device_id={"seq": peer}, device_id_type=pl.DeviceIdType.MESH,
        )

    def first_own():
        return pltpu.make_async_copy(
            out1.at[:, pl.ds(pl.multiple_of(me * col_block, PACK), col_block)],
            got1.at[pl.ds(me * row_block, row_block)], own_sem.at[0],
        )

    def chunk_view(ref, start, count, h, ch):
        return ref.at[
            pl.ds(start, count), pl.ds(h * PACK, PACK), pl.ds(ch * LANES, LANES)
        ]

    lane_parts = width // LANES
    chunks = [(h, ch) for h in range(row_block // PACK) for ch in range(lane_parts)]

    def send_second(index, peer):
        h, ch = chunks[index]
        return pltpu.make_async_remote_copy(
            src_ref=out2.at[
                :, pl.ds(pl.multiple_of(peer * row_block + h * PACK, PACK), PACK),
                pl.ds(ch * LANES, LANES),
            ],
            dst_ref=chunk_view(got2, me * col_block, col_block, h, ch),
            send_sem=send2.at[index], recv_sem=recv2.at[index],
            device_id={"seq": peer}, device_id_type=pl.DeviceIdType.MESH,
        )

    def second_own():
        return pltpu.make_async_copy(
            out2.at[:, pl.ds(pl.multiple_of(me * row_block, PACK), row_block)],
            got2.at[pl.ds(me * col_block, col_block)], own_sem.at[1],
        )

    def to_all(send, index):
        def body(d, carry):
            send(index, hop(d)).start()
            return carry

        lax.fori_loop(1, n, body, 0)

    def await_first(sem):
        view = got1.at[pl.ds(0, (n - 1) * part)]
        pltpu.make_async_copy(view, view, sem).wait()

    def await_second(index, sem):
        h, ch = chunks[index]
        view = chunk_view(got2, 0, (n - 1) * col_block, h, ch)
        pltpu.make_async_copy(view, view, sem).wait()

    for group in range(GROUPS):
        def inner_step(step, slot):
            out1[group * part + step] = dot_nt(a_ref[...], x_buf[slot]).astype(BF16)

        stream(part, [lambda s, slot, group=group: load_x(group * part + s, slot)], inner_step)
        if group == 0:
            pl.semaphore_wait(barrier, n - 1)
        to_all(send_first, group)
    first_own().start()

    def back_step(step, slot):
        mg = (g_buf[slot].astype(F32) * q_buf[slot].astype(F32)).astype(BF16)
        out2[step] = dot_nt(bt_ref[...], mg).astype(BF16)

    stream(col_block, [load_g, load_q], back_step)
    second_own().start()

    acc1[...] = jnp.zeros_like(acc1)
    acc2[...] = jnp.zeros_like(acc2)

    for group in range(GROUPS - 1):
        await_first(recv1.at[group])
    early = max(len(chunks) // 2, 1)
    for index in range(early):
        to_all(send_second, index)
    await_first(recv1.at[GROUPS - 1])
    first_own().wait()

    def turn(got, h, ch, slot, total):
        def body(block, carry):
            start = pl.multiple_of(block * 8, 8)
            value = got[pl.ds(start, 8), pl.ds(h * PACK, PACK), pl.ds(ch * LANES, LANES)]
            turned[slot, pl.ds(pl.multiple_of(block * 8 * PACK, 8 * PACK), 8 * PACK), :] = (
                value.astype(F32).reshape(8 * PACK, LANES)
            )
            return carry

        lax.fori_loop(0, total // 8, body, 0)

    def pick(slot, step, total):
        return turned[slot, pl.ds(step, total, stride=PACK), :].astype(BF16)

    later = list(range(early, len(chunks)))
    halves = col_block // PACK
    for h in range(halves):
        for ch in range(lane_parts):
            turn(got1, h, ch, ch, rows)

        def gate_step(step, slot):
            g = g_buf[slot].astype(F32)
            mg = (g * q_buf[slot].astype(F32)).astype(BF16)
            inner = jnp.concatenate([pick(ch, step, rows) for ch in range(lane_parts)], axis=1)
            y_buf[slot] = (g * dot_tn(inner, bt_ref[...])).astype(BF16)
            acc2[...] += dot_nn(inner, mg)

        def store_dq(step, slot):
            return pltpu.make_async_copy(
                y_buf.at[slot],
                dq_hbm.at[:, pl.ds(pl.multiple_of((h * PACK + step) * rows, LANES), rows)],
                y_sem.at[slot],
            )

        stream(
            PACK,
            [lambda s, slot: load_g(h * PACK + s, slot), lambda s, slot: load_q(h * PACK + s, slot)],
            gate_step, store_dq,
        )
        share = later if h == halves - 1 else later[: max(len(later) // 2, 0)]
        for index in share:
            to_all(send_second, index)
        later = [index for index in later if index not in share]

    second_own().wait()
    for index, (h, ch) in enumerate(chunks):
        await_second(index, recv2.at[index])
        turn(got2, h, ch, 0, cols)
        span = pl.ds(ch * LANES, LANES)

        def block(ref, step):
            start = pl.multiple_of((h * PACK + step) * cols, LANES)
            return ref.at[span, pl.ds(start, cols)]

        def load_part(step, slot):
            return pltpu.make_async_copy(
                block(x_hbm, step), x_buf.at[slot, pl.ds(0, LANES)], x_sem.at[slot]
            )

        def store_part(step, slot):
            return pltpu.make_async_copy(
                y_buf.at[slot, pl.ds(0, LANES)], block(dx_hbm, step), y_sem.at[slot]
            )

        def input_step(step, slot):
            inner_grad = pick(0, step, cols)
            y_buf[slot, pl.ds(0, LANES)] = dot_tn(inner_grad, a_ref[...]).astype(BF16)
            acc1[...] += dot_nn(inner_grad, x_buf[slot, pl.ds(0, LANES)])

        stream(PACK, [load_part], input_step, store_part)

    for group in range(GROUPS):
        await_first(send1.at[group])
    for index in range(len(chunks)):
        await_second(index, send2.at[index])


def fused(inputs, gate_acts, out_grad, first_factor, second_factor):
    n = lax.axis_size("seq")
    width, extent = inputs.shape
    cols, rows = first_factor.shape[0], second_factor.shape[0]
    row_block, col_block = rows // n, cols // n
    chunk_count = (row_block // PACK) * (width // LANES)
    vmem = pl.BlockSpec(memory_space=pltpu.VMEM)
    hbm = pl.BlockSpec(memory_space=pl.ANY)
    dma = pltpu.SemaphoreType.DMA
    long_side = max(rows, cols)
    flops = 12 * width * row_block * cols * rows
    return pl.pallas_call(
        functools.partial(kernel, n),
        out_shape=(
            jax.ShapeDtypeStruct((width, extent), BF16),
            jax.ShapeDtypeStruct((width, extent), BF16),
            jax.ShapeDtypeStruct((cols, cols), F32),
            jax.ShapeDtypeStruct((rows, rows), F32),
        ),
        in_specs=[hbm, hbm, hbm, vmem, vmem],
        out_specs=(hbm, hbm, vmem, vmem),
        scratch_shapes=[
            pltpu.VMEM((row_block, cols, width), BF16),
            pltpu.VMEM((col_block, rows, width), BF16),
            pltpu.VMEM((rows, col_block, width), BF16),
            pltpu.VMEM((cols, row_block, width), BF16),
            pltpu.VMEM((width // LANES, long_side * PACK, LANES), F32),
            pltpu.VMEM((2, width, cols), BF16),
            pltpu.VMEM((2, width, rows), BF16),
            pltpu.VMEM((2, width, rows), BF16),
            pltpu.VMEM((2, width, long_side), BF16),
            dma((2,)), dma((2,)), dma((2,)), dma((2,)), dma((2,)),
            dma((GROUPS,)), dma((GROUPS,)), dma((chunk_count,)), dma((chunk_count,)),
        ],
        compiler_params=pltpu.CompilerParams(
            collective_id=0, has_side_effects=True, vmem_limit_bytes=56 * 2**20
        ),
        cost_estimate=pl.CostEstimate(flops=flops, bytes_accessed=16 * width * extent, transcendentals=0),
    )(inputs, gate_acts, out_grad, first_factor, second_factor.T)


def plain(inputs, gate_acts, out_grad, first_factor, second_factor):
    n = lax.axis_size("seq")
    width, extent = inputs.shape
    cols, rows = first_factor.shape[0], second_factor.shape[0]
    row_block, col_block = rows // n, cols // n
    grid = inputs.reshape(width, row_block, cols)
    first = first_factor.reshape(n, col_block, cols)
    second = second_factor.reshape(rows, n, row_block)

    def exchange(value):
        sent = lax.all_to_all(
            value.reshape(n, -1), "seq", split_axis=0, concat_axis=0, tiled=True
        )
        return sent.reshape(n, col_block, row_block, width)

    def einsum(spec, lhs, rhs):
        return jnp.einsum(spec, lhs, rhs, preferred_element_type=F32)

    received = exchange(einsum("cij,skj->skic", grid, first).astype(BF16))
    mixed = einsum("odgi,fog->idf", received, second)
    g = out_grad.reshape(width, col_block, rows).astype(F32)
    gate_grad = (g * mixed).astype(BF16).reshape(width, extent)
    mg = (g * gate_acts.reshape(width, col_block, rows).astype(F32)).astype(BF16)
    returned = exchange(einsum("vph,hox->opxv", mg, second).astype(BF16))
    second_term = einsum("wjq,ajtw->qat", mg, received).reshape(rows, rows)
    input_grad = einsum("skrc,skj->crj", returned, first).astype(BF16).reshape(width, extent)
    first_term = einsum("skrc,crj->skj", returned, grid).reshape(cols, cols)
    return input_grad, gate_grad, first_term, second_term


def local(inputs, gate_acts, out_grad, first_factor, second_factor):
    n = lax.axis_size("seq")
    width = inputs.shape[0]
    cols, rows = first_factor.shape[0], second_factor.shape[0]
    fits = width % LANES == 0 and rows % (n * PACK) == 0 and cols % (n * PACK) == 0
    args = (inputs, gate_acts, out_grad, first_factor, second_factor)
    if fits:
        input_grad, gate_grad, first_term, second_term = fused(*args)
        second_term = second_term.T
    else:
        input_grad, gate_grad, first_term, second_term = plain(*args)
    totals = lax.psum((first_term, second_term), "chan")
    first_grad = lax.psum_scatter(totals[0], "seq", scatter_dimension=0, tiled=True)
    second_grad = lax.psum_scatter(totals[1], "seq", scatter_dimension=0, tiled=True)
    return input_grad, gate_grad, first_grad, second_grad


def solution(mesh):
    return jax.shard_map(
        local,
        mesh=mesh,
        in_specs=(P("chan", "seq"), P("chan", "seq"), P("chan", "seq"), P(), P()),
        out_specs=(P("chan", "seq"), P("chan", "seq"), P("seq", None), P("seq", None)),
        check_vma=False,
    )
```

```python
import functools

import jax
import jax.numpy as jnp
from jax import lax
from jax.experimental import pallas as pl
from jax.experimental.pallas import tpu as pltpu
from jax.sharding import PartitionSpec as P

BF16 = jnp.bfloat16
F32 = jnp.float32
LANES = 128
PACK = 16
GROUPS = 8


def dot_nn(lhs, rhs):
    return lax.dot_general(lhs, rhs, (((1,), (0,)), ((), ())), preferred_element_type=F32)


def dot_nt(lhs, rhs):
    return lax.dot_general(lhs, rhs, (((1,), (1,)), ((), ())), preferred_element_type=F32)


def dot_tn(lhs, rhs):
    return lax.dot_general(lhs, rhs, (((0,), (0,)), ((), ())), preferred_element_type=F32)


def stream(count, loads, work, store=None):
    def body(step, carry):
        slot = lax.rem(step, 2)

        @pl.when(step + 1 < count)
        def _():
            for load in loads:
                load(step + 1, 1 - slot).start()

        for load in loads:
            load(step, slot).wait()
        if store is not None:

            @pl.when(step >= 2)
            def _():
                store(step - 2, slot).wait()

        work(step, slot)
        if store is not None:
            store(step, slot).start()
        return carry

    for load in loads:
        load(0, 0).start()
    lax.fori_loop(0, count, body, 0)
    if store is not None:
        for step in range(max(count - 2, 0), count):
            store(step, step % 2).wait()


def kernel(
    n, chans, low, x_hbm, q_hbm, g_hbm, a_ref, b_ref,
    dx_hbm, dq_hbm, d1_ref, d2_ref,
    out1, out2, got1, got2, turned, x_buf, g_buf, q_buf, y_buf, bt_ref, acc1, acc2,
    terms, land1, sums, land2, final,
    x_sem, g_sem, q_sem, y_sem, own_sem, send1, recv1, send2, recv2, send_sum, recv_sum,
):
    me, my_chan = lax.axis_index("seq"), lax.axis_index("chan")
    width = x_hbm.shape[0]
    rows, cols = b_ref.shape[0], a_ref.shape[0]
    row_block, col_block = rows // n, cols // n
    part = row_block // GROUPS

    def hop(d):
        return lax.rem(me + d, n)

    near, high = low * chans, n // low
    my_low, my_high = lax.rem(me, low), me // low
    my_near = my_low * chans + my_chan

    def near_device(d):
        slot = lax.rem(my_near + d, near)
        return slot, {"seq": my_high * low + slot // chans, "chan": lax.rem(slot, chans)}

    def remote(src, dst, kind, which, device):
        return pltpu.make_async_remote_copy(
            src_ref=src, dst_ref=dst,
            send_sem=send_sum.at[kind, which], recv_sem=recv_sum.at[kind, which],
            device_id=device, device_id_type=pl.DeviceIdType.MESH,
        )

    def await_sum(view, kind, which):
        pltpu.make_async_copy(view, view, recv_sum.at[kind, which]).wait()
        pltpu.make_async_copy(view, view, send_sum.at[kind, which]).wait()

    def sum_near_start(which):
        def body(d, carry):
            slot, device = near_device(d)
            remote(
                terms.at[which, slot], land1.at[which, my_near], 0, which, device
            ).start()
            return carry

        lax.fori_loop(1, near, body, 0)

    def sum_far_start(which):
        await_sum(land1.at[which, pl.ds(0, near - 1)], 0, which)
        sums[which] = terms[which, my_near]

        def add(d, carry):
            sums[which] += land1[which, lax.rem(my_near + d, near)]
            return carry

        lax.fori_loop(1, near, add, 0)

        def body(d, carry):
            to = lax.rem(my_high + d, high)
            remote(
                sums.at[which, to], land2.at[which, my_high], 1, which,
                {"seq": to * low + my_low, "chan": my_chan},
            ).start()
            return carry

        lax.fori_loop(1, high, body, 0)

    def sum_share_start(which):
        await_sum(land2.at[which, pl.ds(0, high - 1)], 1, which)
        final[which, my_chan] = sums[which, my_high]

        def add(d, carry):
            final[which, my_chan] += land2[which, lax.rem(my_high + d, high)]
            return carry

        lax.fori_loop(1, high, add, 0)

        def body(d, carry):
            remote(
                final.at[which, my_chan], final.at[which, my_chan], 2, which,
                {"seq": me, "chan": lax.rem(my_chan + d, chans)},
            ).start()
            return carry

        lax.fori_loop(1, chans, body, 0)

    def sum_end(which, out):
        await_sum(final.at[which, pl.ds(0, chans - 1)], 2, which)
        out[...] = final[which].reshape(out.shape)

    def put_terms(which, strip, value):
        share = row_block // chans
        for c in range(chans):
            terms[which, (strip % low) * chans + c, strip // low] = value[c * share:(c + 1) * share]

    barrier = pltpu.get_barrier_semaphore()

    def greet(d, carry):
        pl.semaphore_signal(
            barrier, inc=1, device_id={"seq": hop(d)}, device_id_type=pl.DeviceIdType.MESH
        )
        return carry

    lax.fori_loop(1, n, greet, 0)

    def greet_chan(d, carry):
        def body(spot, inner):
            pl.semaphore_signal(
                barrier, inc=1,
                device_id={"seq": my_high * low + spot, "chan": lax.rem(my_chan + d, chans)},
                device_id_type=pl.DeviceIdType.MESH,
            )
            return inner

        return lax.fori_loop(0, low, body, carry)

    lax.fori_loop(1, chans, greet_chan, 0)

    def load_x(step, slot):
        return pltpu.make_async_copy(
            x_hbm.at[:, pl.ds(pl.multiple_of(step * cols, LANES), cols)],
            x_buf.at[slot], x_sem.at[slot],
        )

    def load_g(step, slot):
        return pltpu.make_async_copy(
            g_hbm.at[:, pl.ds(pl.multiple_of(step * rows, LANES), rows)],
            g_buf.at[slot], g_sem.at[slot],
        )

    def load_q(step, slot):
        return pltpu.make_async_copy(
            q_hbm.at[:, pl.ds(pl.multiple_of(step * rows, LANES), rows)],
            q_buf.at[slot], q_sem.at[slot],
        )

    def send_first(group, peer):
        return pltpu.make_async_remote_copy(
            src_ref=out1.at[
                pl.ds(group * part, part), pl.ds(pl.multiple_of(peer * col_block, PACK), col_block)
            ],
            dst_ref=got1.at[pl.ds(me * row_block + group * part, part)],
            send_sem=send1.at[group], recv_sem=recv1.at[group],
            device_id={"seq": peer}, device_id_type=pl.DeviceIdType.MESH,
        )

    def first_own():
        return pltpu.make_async_copy(
            out1.at[:, pl.ds(pl.multiple_of(me * col_block, PACK), col_block)],
            got1.at[pl.ds(me * row_block, row_block)], own_sem.at[0],
        )

    def chunk_view(ref, start, count, h, ch):
        return ref.at[
            pl.ds(start, count), pl.ds(h * PACK, PACK), pl.ds(ch * LANES, LANES)
        ]

    lane_parts = width // LANES
    chunks = [(h, ch) for h in range(row_block // PACK) for ch in range(lane_parts)]

    def send_second(index, peer):
        h, ch = chunks[index]
        return pltpu.make_async_remote_copy(
            src_ref=out2.at[
                :, pl.ds(pl.multiple_of(peer * row_block + h * PACK, PACK), PACK),
                pl.ds(ch * LANES, LANES),
            ],
            dst_ref=chunk_view(got2, me * col_block, col_block, h, ch),
            send_sem=send2.at[index], recv_sem=recv2.at[index],
            device_id={"seq": peer}, device_id_type=pl.DeviceIdType.MESH,
        )

    def second_own():
        return pltpu.make_async_copy(
            out2.at[:, pl.ds(pl.multiple_of(me * row_block, PACK), row_block)],
            got2.at[pl.ds(me * col_block, col_block)], own_sem.at[1],
        )

    def to_all(send, index):
        def body(d, carry):
            send(index, hop(d)).start()
            return carry

        lax.fori_loop(1, n, body, 0)

    def await_first(sem):
        view = got1.at[pl.ds(0, (n - 1) * part)]
        pltpu.make_async_copy(view, view, sem).wait()

    def await_second(index, sem):
        h, ch = chunks[index]
        view = chunk_view(got2, 0, (n - 1) * col_block, h, ch)
        pltpu.make_async_copy(view, view, sem).wait()

    def inner_step(first, step, slot):
        out1[first + step] = dot_nt(a_ref[...], x_buf[slot]).astype(BF16)

    stream(part, [load_x], functools.partial(inner_step, 0))
    pl.semaphore_wait(barrier, n - 1 + low * (chans - 1))
    to_all(send_first, 0)

    def inner_send_step(step, slot):
        inner_step(part, step, slot)

        @pl.when(lax.rem(step, part) == part - 1)
        def _():
            to_all(send_first, step // part + 1)

    stream(row_block - part, [lambda s, slot: load_x(part + s, slot)], inner_send_step)
    first_own().start()

    for strip in range(rows // LANES):
        span = pl.ds(strip * LANES, LANES)
        bt_ref[span, :] = b_ref[:, span].T

    def back_step(step, slot):
        mg = (g_buf[slot].astype(F32) * q_buf[slot].astype(F32)).astype(BF16)
        out2[step] = dot_nt(bt_ref[...], mg).astype(BF16)

    stream(col_block, [load_g, load_q], back_step)
    second_own().start()

    acc1[...] = jnp.zeros_like(acc1)
    acc2[...] = jnp.zeros_like(acc2)

    for group in range(GROUPS - 1):
        await_first(recv1.at[group])
    early = max(len(chunks) // 2, 1)
    for index in range(early):
        to_all(send_second, index)
    await_first(recv1.at[GROUPS - 1])
    first_own().wait()

    def turn(got, h, ch, slot, total):
        def body(block, carry):
            start = pl.multiple_of(block * 8, 8)
            value = got[pl.ds(start, 8), pl.ds(h * PACK, PACK), pl.ds(ch * LANES, LANES)]
            turned[slot, pl.ds(pl.multiple_of(block * 8 * PACK, 8 * PACK), 8 * PACK), :] = (
                value.astype(F32).reshape(8 * PACK, LANES)
            )
            return carry

        lax.fori_loop(0, total // 8, body, 0)

    def pick(slot, step, total):
        return turned[slot, pl.ds(step, total, stride=PACK), :].astype(BF16)

    later = list(range(early, len(chunks)))
    halves = col_block // PACK
    for h in range(halves):
        for ch in range(lane_parts):
            turn(got1, h, ch, ch, rows)

        def gate_step(step, slot):
            g = g_buf[slot].astype(F32)
            mg = (g * q_buf[slot].astype(F32)).astype(BF16)
            inner = jnp.concatenate([pick(ch, step, rows) for ch in range(lane_parts)], axis=1)
            y_buf[slot] = (g * dot_tn(inner, bt_ref[...])).astype(BF16)
            acc2[...] += dot_nn(inner, mg)

        def store_dq(step, slot):
            return pltpu.make_async_copy(
                y_buf.at[slot],
                dq_hbm.at[:, pl.ds(pl.multiple_of((h * PACK + step) * rows, LANES), rows)],
                y_sem.at[slot],
            )

        stream(
            PACK,
            [lambda s, slot: load_g(h * PACK + s, slot), lambda s, slot: load_q(h * PACK + s, slot)],
            gate_step, store_dq,
        )
        share = later if h == halves - 1 else later[: max(len(later) // 2, 0)]
        for index in share:
            to_all(send_second, index)
        later = [index for index in later if index not in share]

    for strip in range(rows // LANES):
        value = acc2[:, pl.ds(strip * LANES, LANES)].T
        for b in range(LANES // row_block):
            put_terms(1, strip * (LANES // row_block) + b, value[b * row_block:(b + 1) * row_block])
    sum_near_start(1)

    second_own().wait()
    for index, (h, ch) in enumerate(chunks):
        await_second(index, recv2.at[index])
        turn(got2, h, ch, 0, cols)
        span = pl.ds(ch * LANES, LANES)

        def block(ref, step):
            start = pl.multiple_of((h * PACK + step) * cols, LANES)
            return ref.at[span, pl.ds(start, cols)]

        def load_part(step, slot):
            return pltpu.make_async_copy(
                block(x_hbm, step), x_buf.at[slot, pl.ds(0, LANES)], x_sem.at[slot]
            )

        def store_part(step, slot):
            return pltpu.make_async_copy(
                y_buf.at[slot, pl.ds(0, LANES)], block(dx_hbm, step), y_sem.at[slot]
            )

        def term_step(step, slot):
            acc1[...] += dot_nn(pick(0, step, cols), x_buf[slot, pl.ds(0, LANES)])

        def input_step(step, slot):
            y_buf[slot, pl.ds(0, LANES)] = dot_tn(pick(0, step, cols), a_ref[...]).astype(BF16)

        def both_steps(step, slot):
            input_step(step, slot)
            term_step(step, slot)

        if index < len(chunks) - 1:
            stream(PACK, [load_part], both_steps, store_part)
        else:
            stream(PACK, [load_part], term_step)
            for strip in range(n):
                put_terms(0, strip, acc1[pl.ds(strip * row_block, row_block), :])
            sum_near_start(0)
            stream(PACK, [], input_step, store_part)
        if index == 0:
            sum_far_start(1)
        if index == min(1, len(chunks) - 1):
            sum_share_start(1)

    sum_far_start(0)
    sum_share_start(0)
    sum_end(1, d2_ref)
    sum_end(0, d1_ref)

    for group in range(GROUPS):
        await_first(send1.at[group])
    for index in range(len(chunks)):
        await_second(index, send2.at[index])


def fused(inputs, gate_acts, out_grad, first_factor, second_factor):
    n = lax.axis_size("seq")
    width, extent = inputs.shape
    cols, rows = first_factor.shape[0], second_factor.shape[0]
    row_block, col_block = rows // n, cols // n
    chans = lax.axis_size("chan")
    low = max(d for d in range(1, n + 1) if n % d == 0 and d * d <= n)
    near, high, share = low * chans, n // low, row_block // chans
    chunk_count = (row_block // PACK) * (width // LANES)
    vmem = pl.BlockSpec(memory_space=pltpu.VMEM)
    hbm = pl.BlockSpec(memory_space=pl.ANY)
    dma = pltpu.SemaphoreType.DMA
    long_side = max(rows, cols)
    flops = 12 * width * row_block * cols * rows
    return pl.pallas_call(
        functools.partial(kernel, n, chans, low),
        out_shape=(
            jax.ShapeDtypeStruct((width, extent), BF16),
            jax.ShapeDtypeStruct((width, extent), BF16),
            jax.ShapeDtypeStruct((cols // n, cols), F32),
            jax.ShapeDtypeStruct((rows // n, rows), F32),
        ),
        in_specs=[hbm, hbm, hbm, vmem, vmem],
        out_specs=(hbm, hbm, vmem, vmem),
        scratch_shapes=[
            pltpu.VMEM((row_block, cols, width), BF16),
            pltpu.VMEM((col_block, rows, width), BF16),
            pltpu.VMEM((rows, col_block, width), BF16),
            pltpu.VMEM((cols, row_block, width), BF16),
            pltpu.VMEM((width // LANES, long_side * PACK, LANES), F32),
            pltpu.VMEM((2, width, cols), BF16),
            pltpu.VMEM((2, width, rows), BF16),
            pltpu.VMEM((2, width, rows), BF16),
            pltpu.VMEM((2, width, long_side), BF16),
            pltpu.VMEM((rows, rows), BF16),
            pltpu.VMEM((cols, cols), F32),
            pltpu.VMEM((rows, rows), F32),
            pltpu.VMEM((2, near, high, share, long_side), F32),
            pltpu.VMEM((2, near, high, share, long_side), F32),
            pltpu.VMEM((2, high, share, long_side), F32),
            pltpu.VMEM((2, high, share, long_side), F32),
            pltpu.VMEM((2, chans, share, long_side), F32),
            dma((2,)), dma((2,)), dma((2,)), dma((2,)), dma((2,)),
            dma((GROUPS,)), dma((GROUPS,)), dma((chunk_count,)), dma((chunk_count,)),
            dma((3, 2)), dma((3, 2)),
        ],
        compiler_params=pltpu.CompilerParams(
            collective_id=0, has_side_effects=True, vmem_limit_bytes=58 * 2**20
        ),
        cost_estimate=pl.CostEstimate(flops=flops, bytes_accessed=16 * width * extent, transcendentals=0),
    )(inputs, gate_acts, out_grad, first_factor, second_factor)


def plain(inputs, gate_acts, out_grad, first_factor, second_factor):
    n = lax.axis_size("seq")
    width, extent = inputs.shape
    cols, rows = first_factor.shape[0], second_factor.shape[0]
    row_block, col_block = rows // n, cols // n
    grid = inputs.reshape(width, row_block, cols)
    first = first_factor.reshape(n, col_block, cols)
    second = second_factor.reshape(rows, n, row_block)

    def exchange(value):
        sent = lax.all_to_all(
            value.reshape(n, -1), "seq", split_axis=0, concat_axis=0, tiled=True
        )
        return sent.reshape(n, col_block, row_block, width)

    def einsum(spec, lhs, rhs):
        return jnp.einsum(spec, lhs, rhs, preferred_element_type=F32)

    received = exchange(einsum("cij,skj->skic", grid, first).astype(BF16))
    mixed = einsum("odgi,fog->idf", received, second)
    g = out_grad.reshape(width, col_block, rows).astype(F32)
    gate_grad = (g * mixed).astype(BF16).reshape(width, extent)
    mg = (g * gate_acts.reshape(width, col_block, rows).astype(F32)).astype(BF16)
    returned = exchange(einsum("vph,hox->opxv", mg, second).astype(BF16))
    second_term = einsum("wjq,ajtw->qat", mg, received).reshape(rows, rows)
    input_grad = einsum("skrc,skj->crj", returned, first).astype(BF16).reshape(width, extent)
    first_term = einsum("skrc,crj->skj", returned, grid).reshape(cols, cols)
    return input_grad, gate_grad, first_term, second_term


def local(inputs, gate_acts, out_grad, first_factor, second_factor):
    n = lax.axis_size("seq")
    width = inputs.shape[0]
    cols, rows = first_factor.shape[0], second_factor.shape[0]
    chans = lax.axis_size("chan")
    fits = (
        rows == cols
        and width % LANES == 0
        and rows % (n * PACK) == 0
        and LANES % (rows // n) == 0
        and rows % (n * chans * 8) == 0
        and chans > 1
        and n >= 4
    )
    args = (inputs, gate_acts, out_grad, first_factor, second_factor)
    if fits:
        return fused(*args)
    input_grad, gate_grad, first_term, second_term = plain(*args)
    totals = lax.psum((first_term, second_term), "chan")
    first_grad = lax.psum_scatter(totals[0], "seq", scatter_dimension=0, tiled=True)
    second_grad = lax.psum_scatter(totals[1], "seq", scatter_dimension=0, tiled=True)
    return input_grad, gate_grad, first_grad, second_grad


def solution(mesh):
    return jax.shard_map(
        local,
        mesh=mesh,
        in_specs=(P("chan", "seq"), P("chan", "seq"), P("chan", "seq"), P(), P()),
        out_specs=(P("chan", "seq"), P("chan", "seq"), P("seq", None), P("seq", None)),
        check_vma=False,
    )
```

```python
import functools

import jax
import jax.numpy as jnp
from jax import lax
from jax.experimental import pallas as pl
from jax.experimental.pallas import tpu as pltpu
from jax.sharding import PartitionSpec as P

BF16 = jnp.bfloat16
F32 = jnp.float32
LANES = 128
PACK = 16
GROUPS = 8


def dot_nn(lhs, rhs):
    return lax.dot_general(lhs, rhs, (((1,), (0,)), ((), ())), preferred_element_type=F32)


def dot_nt(lhs, rhs):
    return lax.dot_general(lhs, rhs, (((1,), (1,)), ((), ())), preferred_element_type=F32)


def dot_tn(lhs, rhs):
    return lax.dot_general(lhs, rhs, (((0,), (0,)), ((), ())), preferred_element_type=F32)


def stream(count, loads, work, store=None):
    def body(step, carry):
        slot = lax.rem(step, 2)

        @pl.when(step + 1 < count)
        def _():
            for load in loads:
                load(step + 1, 1 - slot).start()

        for load in loads:
            load(step, slot).wait()
        if store is not None:

            @pl.when(step >= 2)
            def _():
                store(step - 2, slot).wait()

        work(step, slot)
        if store is not None:
            store(step, slot).start()
        return carry

    for load in loads:
        load(0, 0).start()
    lax.fori_loop(0, count, body, 0)
    if store is not None:
        for step in range(max(count - 2, 0), count):
            store(step, step % 2).wait()


def kernel(
    n, chans, low, x_hbm, q_hbm, g_hbm, a_ref, b_ref,
    dx_hbm, dq_hbm, d1_ref, d2_ref,
    out1, out2, got1, got2, turned, x_buf, g_buf, q_buf, y_buf, bt_ref, acc1, acc2,
    terms, land1, sums, land2, final,
    x_sem, g_sem, q_sem, y_sem, own_sem, send1, recv1, send2, recv2, send_sum, recv_sum,
):
    me, my_chan = lax.axis_index("seq"), lax.axis_index("chan")
    width = x_hbm.shape[0]
    rows, cols = b_ref.shape[0], a_ref.shape[0]
    row_block, col_block = rows // n, cols // n
    part = row_block // GROUPS

    def hop(d):
        return lax.rem(me + d, n)

    near, high = low * chans, n // low
    my_low, my_high = lax.rem(me, low), me // low
    my_near = my_low * chans + my_chan

    def near_device(d):
        slot = lax.rem(my_near + d, near)
        return slot, {"seq": my_high * low + slot // chans, "chan": lax.rem(slot, chans)}

    def remote(src, dst, kind, which, device):
        return pltpu.make_async_remote_copy(
            src_ref=src, dst_ref=dst,
            send_sem=send_sum.at[kind, which], recv_sem=recv_sum.at[kind, which],
            device_id=device, device_id_type=pl.DeviceIdType.MESH,
        )

    def await_sum(view, kind, which):
        pltpu.make_async_copy(view, view, recv_sum.at[kind, which]).wait()
        pltpu.make_async_copy(view, view, send_sum.at[kind, which]).wait()

    def sum_near_start(which):
        def body(d, carry):
            slot, device = near_device(d)
            remote(
                terms.at[which, slot], land1.at[which, my_near], 0, which, device
            ).start()
            return carry

        lax.fori_loop(1, near, body, 0)

    def sum_far_start(which):
        await_sum(land1.at[which, pl.ds(0, near - 1)], 0, which)
        sums[which] = terms[which, my_near]

        def add(d, carry):
            sums[which] += land1[which, lax.rem(my_near + d, near)]
            return carry

        lax.fori_loop(1, near, add, 0)

        def body(d, carry):
            to = lax.rem(my_high + d, high)
            remote(
                sums.at[which, to], land2.at[which, my_high], 1, which,
                {"seq": to * low + my_low, "chan": my_chan},
            ).start()
            return carry

        lax.fori_loop(1, high, body, 0)

    def sum_share_start(which):
        await_sum(land2.at[which, pl.ds(0, high - 1)], 1, which)
        final[which, my_chan] = sums[which, my_high]

        def add(d, carry):
            final[which, my_chan] += land2[which, lax.rem(my_high + d, high)]
            return carry

        lax.fori_loop(1, high, add, 0)

        def body(d, carry):
            remote(
                final.at[which, my_chan], final.at[which, my_chan], 2, which,
                {"seq": me, "chan": lax.rem(my_chan + d, chans)},
            ).start()
            return carry

        lax.fori_loop(1, chans, body, 0)

    def sum_end(which, out):
        await_sum(final.at[which, pl.ds(0, chans - 1)], 2, which)
        out[...] = final[which].reshape(out.shape)

    def put_terms(which, strip, value):
        share = row_block // chans
        for c in range(chans):
            terms[which, (strip % low) * chans + c, strip // low] = value[c * share:(c + 1) * share]

    barrier = pltpu.get_barrier_semaphore()

    def greet(d, carry):
        pl.semaphore_signal(
            barrier, inc=1, device_id={"seq": hop(d)}, device_id_type=pl.DeviceIdType.MESH
        )
        return carry

    lax.fori_loop(1, n, greet, 0)

    def greet_chan(d, carry):
        def body(spot, inner):
            pl.semaphore_signal(
                barrier, inc=1,
                device_id={"seq": my_high * low + spot, "chan": lax.rem(my_chan + d, chans)},
                device_id_type=pl.DeviceIdType.MESH,
            )
            return inner

        return lax.fori_loop(0, low, body, carry)

    lax.fori_loop(1, chans, greet_chan, 0)

    def load_x(step, slot):
        return pltpu.make_async_copy(
            x_hbm.at[:, pl.ds(pl.multiple_of(step * cols, LANES), cols)],
            x_buf.at[slot], x_sem.at[slot],
        )

    def load_g(step, slot):
        return pltpu.make_async_copy(
            g_hbm.at[:, pl.ds(pl.multiple_of(step * rows, LANES), rows)],
            g_buf.at[slot], g_sem.at[slot],
        )

    def load_q(step, slot):
        return pltpu.make_async_copy(
            q_hbm.at[:, pl.ds(pl.multiple_of(step * rows, LANES), rows)],
            q_buf.at[slot], q_sem.at[slot],
        )

    def send_first(group, peer):
        return pltpu.make_async_remote_copy(
            src_ref=out1.at[
                pl.ds(group * part, part), pl.ds(pl.multiple_of(peer * col_block, PACK), col_block)
            ],
            dst_ref=got1.at[pl.ds(me * row_block + group * part, part)],
            send_sem=send1.at[group], recv_sem=recv1.at[group],
            device_id={"seq": peer}, device_id_type=pl.DeviceIdType.MESH,
        )

    def first_own():
        return pltpu.make_async_copy(
            out1.at[:, pl.ds(pl.multiple_of(me * col_block, PACK), col_block)],
            got1.at[pl.ds(me * row_block, row_block)], own_sem.at[0],
        )

    def chunk_view(ref, start, count, h, ch):
        return ref.at[
            pl.ds(start, count), pl.ds(h * PACK, PACK), pl.ds(ch * LANES, LANES)
        ]

    lane_parts = width // LANES
    chunks = [(h, ch) for h in range(row_block // PACK) for ch in range(lane_parts)]

    def send_second(index, peer):
        h, ch = chunks[index]
        return pltpu.make_async_remote_copy(
            src_ref=out2.at[
                :, pl.ds(pl.multiple_of(peer * row_block + h * PACK, PACK), PACK),
                pl.ds(ch * LANES, LANES),
            ],
            dst_ref=chunk_view(got2, me * col_block, col_block, h, ch),
            send_sem=send2.at[index], recv_sem=recv2.at[index],
            device_id={"seq": peer}, device_id_type=pl.DeviceIdType.MESH,
        )

    def second_own():
        return pltpu.make_async_copy(
            out2.at[:, pl.ds(pl.multiple_of(me * row_block, PACK), row_block)],
            got2.at[pl.ds(me * col_block, col_block)], own_sem.at[1],
        )

    def to_all(send, index):
        def body(t, carry):
            d = (1 - lax.rem(t, 2)) * (n // 2) + (t + 1) // 2
            send(index, hop(d)).start()
            return carry

        lax.fori_loop(0, n - 1, body, 0)

    def await_first(sem):
        view = got1.at[pl.ds(0, (n - 1) * part)]
        pltpu.make_async_copy(view, view, sem).wait()

    def await_second(index, sem):
        h, ch = chunks[index]
        view = chunk_view(got2, 0, (n - 1) * col_block, h, ch)
        pltpu.make_async_copy(view, view, sem).wait()

    def inner_step(first, step, slot):
        out1[first + step] = dot_nt(a_ref[...], x_buf[slot]).astype(BF16)

    stream(part, [load_x], functools.partial(inner_step, 0))
    pl.semaphore_wait(barrier, n - 1 + low * (chans - 1))
    to_all(send_first, 0)

    def inner_send_step(step, slot):
        inner_step(part, step, slot)

        @pl.when(lax.rem(step, part) == part - 1)
        def _():
            to_all(send_first, step // part + 1)

    stream(row_block - part, [lambda s, slot: load_x(part + s, slot)], inner_send_step)
    first_own().start()

    for strip in range(rows // LANES):
        span = pl.ds(strip * LANES, LANES)
        bt_ref[span, :] = b_ref[:, span].T

    def back_step(step, slot):
        mg = (g_buf[slot].astype(F32) * q_buf[slot].astype(F32)).astype(BF16)
        out2[step] = dot_nt(bt_ref[...], mg).astype(BF16)

    stream(col_block, [load_g, load_q], back_step)
    second_own().start()

    acc1[...] = jnp.zeros_like(acc1)
    acc2[...] = jnp.zeros_like(acc2)

    for group in range(GROUPS - 1):
        await_first(recv1.at[group])
    early = max(len(chunks) // 2, 1)
    for index in range(early):
        to_all(send_second, index)
    await_first(recv1.at[GROUPS - 1])
    first_own().wait()

    def turn(got, h, ch, slot, total):
        def body(block, carry):
            start = pl.multiple_of(block * 8, 8)
            value = got[pl.ds(start, 8), pl.ds(h * PACK, PACK), pl.ds(ch * LANES, LANES)]
            turned[slot, pl.ds(pl.multiple_of(block * 8 * PACK, 8 * PACK), 8 * PACK), :] = (
                value.astype(F32).reshape(8 * PACK, LANES)
            )
            return carry

        lax.fori_loop(0, total // 8, body, 0)

    def pick(slot, step, total):
        return turned[slot, pl.ds(step, total, stride=PACK), :].astype(BF16)

    later = list(range(early, len(chunks)))
    halves = col_block // PACK
    for h in range(halves):
        for ch in range(lane_parts):
            turn(got1, h, ch, ch, rows)

        def gate_step(step, slot):
            g = g_buf[slot].astype(F32)
            mg = (g * q_buf[slot].astype(F32)).astype(BF16)
            inner = jnp.concatenate([pick(ch, step, rows) for ch in range(lane_parts)], axis=1)
            y_buf[slot] = (g * dot_tn(inner, bt_ref[...])).astype(BF16)
            acc2[...] += dot_nn(inner, mg)

        def store_dq(step, slot):
            return pltpu.make_async_copy(
                y_buf.at[slot],
                dq_hbm.at[:, pl.ds(pl.multiple_of((h * PACK + step) * rows, LANES), rows)],
                y_sem.at[slot],
            )

        stream(
            PACK,
            [lambda s, slot: load_g(h * PACK + s, slot), lambda s, slot: load_q(h * PACK + s, slot)],
            gate_step, store_dq,
        )
        share = later if h == halves - 1 else later[: max(len(later) // 2, 0)]
        for index in share:
            to_all(send_second, index)
        later = [index for index in later if index not in share]

    for strip in range(rows // LANES):
        value = acc2[:, pl.ds(strip * LANES, LANES)].T
        for b in range(LANES // row_block):
            put_terms(1, strip * (LANES // row_block) + b, value[b * row_block:(b + 1) * row_block])
    sum_near_start(1)

    second_own().wait()
    for index, (h, ch) in enumerate(chunks):
        await_second(index, recv2.at[index])
        turn(got2, h, ch, 0, cols)
        span = pl.ds(ch * LANES, LANES)

        def block(ref, step):
            start = pl.multiple_of((h * PACK + step) * cols, LANES)
            return ref.at[span, pl.ds(start, cols)]

        def load_part(step, slot):
            return pltpu.make_async_copy(
                block(x_hbm, step), x_buf.at[slot, pl.ds(0, LANES)], x_sem.at[slot]
            )

        def store_part(step, slot):
            return pltpu.make_async_copy(
                y_buf.at[slot, pl.ds(0, LANES)], block(dx_hbm, step), y_sem.at[slot]
            )

        def term_step(step, slot):
            acc1[...] += dot_nn(pick(0, step, cols), x_buf[slot, pl.ds(0, LANES)])

        def load_pair(which, sems):
            return lambda step, slot: pltpu.make_async_copy(
                block(x_hbm, 2 * step + which),
                x_buf.at[slot, pl.ds(which * LANES, LANES)], sems.at[slot],
            )

        def pair_step(step, slot):
            both = jnp.concatenate(
                [pick(0, 2 * step, cols), pick(0, 2 * step + 1, cols)], axis=1
            )
            acc1[...] += dot_nn(both, x_buf[slot, pl.ds(0, 2 * LANES)])

        def input_step(step, slot):
            y_buf[slot, pl.ds(0, LANES)] = dot_tn(pick(0, step, cols), a_ref[...]).astype(BF16)

        def both_steps(step, slot):
            input_step(step, slot)
            term_step(step, slot)

        if index < len(chunks) - 1:
            stream(PACK, [load_part], both_steps, store_part)
        else:
            stream(PACK // 2, [load_pair(0, x_sem), load_pair(1, g_sem)], pair_step)
            for strip in range(n):
                put_terms(0, strip, acc1[pl.ds(strip * row_block, row_block), :])
            sum_near_start(0)
            stream(PACK, [], input_step, store_part)
        if index == 0:
            sum_far_start(1)
        if index == min(1, len(chunks) - 1):
            sum_share_start(1)

    sum_far_start(0)
    sum_share_start(0)
    sum_end(1, d2_ref)
    sum_end(0, d1_ref)

    for group in range(GROUPS):
        await_first(send1.at[group])
    for index in range(len(chunks)):
        await_second(index, send2.at[index])


def fused(inputs, gate_acts, out_grad, first_factor, second_factor):
    n = lax.axis_size("seq")
    width, extent = inputs.shape
    cols, rows = first_factor.shape[0], second_factor.shape[0]
    row_block, col_block = rows // n, cols // n
    chans = lax.axis_size("chan")
    low = max(d for d in range(1, n + 1) if n % d == 0 and d * d <= n)
    near, high, share = low * chans, n // low, row_block // chans
    chunk_count = (row_block // PACK) * (width // LANES)
    vmem = pl.BlockSpec(memory_space=pltpu.VMEM)
    hbm = pl.BlockSpec(memory_space=pl.ANY)
    dma = pltpu.SemaphoreType.DMA
    long_side = max(rows, cols)
    flops = 12 * width * row_block * cols * rows
    return pl.pallas_call(
        functools.partial(kernel, n, chans, low),
        out_shape=(
            jax.ShapeDtypeStruct((width, extent), BF16),
            jax.ShapeDtypeStruct((width, extent), BF16),
            jax.ShapeDtypeStruct((cols // n, cols), F32),
            jax.ShapeDtypeStruct((rows // n, rows), F32),
        ),
        in_specs=[hbm, hbm, hbm, vmem, vmem],
        out_specs=(hbm, hbm, vmem, vmem),
        scratch_shapes=[
            pltpu.VMEM((row_block, cols, width), BF16),
            pltpu.VMEM((col_block, rows, width), BF16),
            pltpu.VMEM((rows, col_block, width), BF16),
            pltpu.VMEM((cols, row_block, width), BF16),
            pltpu.VMEM((width // LANES, long_side * PACK, LANES), F32),
            pltpu.VMEM((2, width, cols), BF16),
            pltpu.VMEM((2, width, rows), BF16),
            pltpu.VMEM((2, width, rows), BF16),
            pltpu.VMEM((2, width, long_side), BF16),
            pltpu.VMEM((rows, rows), BF16),
            pltpu.VMEM((cols, cols), F32),
            pltpu.VMEM((rows, rows), F32),
            pltpu.VMEM((2, near, high, share, long_side), F32),
            pltpu.VMEM((2, near, high, share, long_side), F32),
            pltpu.VMEM((2, high, share, long_side), F32),
            pltpu.VMEM((2, high, share, long_side), F32),
            pltpu.VMEM((2, chans, share, long_side), F32),
            dma((2,)), dma((2,)), dma((2,)), dma((2,)), dma((2,)),
            dma((GROUPS,)), dma((GROUPS,)), dma((chunk_count,)), dma((chunk_count,)),
            dma((3, 2)), dma((3, 2)),
        ],
        compiler_params=pltpu.CompilerParams(
            collective_id=0, has_side_effects=True, vmem_limit_bytes=58 * 2**20
        ),
        cost_estimate=pl.CostEstimate(flops=flops, bytes_accessed=16 * width * extent, transcendentals=0),
    )(inputs, gate_acts, out_grad, first_factor, second_factor)


def copy_kernel(a_in, b_in, a_out, b_out):
    a_out[...] = a_in[...]
    b_out[...] = b_in[...]


def hand_out(first, second):
    rows = 2 * PACK
    spec = pl.BlockSpec((rows, first.shape[1]), lambda i: (i, 0))
    return pl.pallas_call(
        copy_kernel,
        out_shape=tuple(jax.ShapeDtypeStruct(v.shape, v.dtype) for v in (first, second)),
        grid=(first.shape[0] // rows,),
        in_specs=[spec, spec],
        out_specs=(spec, spec),
        compiler_params=pltpu.CompilerParams(vmem_limit_bytes=56 * 2**20),
        cost_estimate=pl.CostEstimate(flops=0, bytes_accessed=8 * first.size, transcendentals=0),
    )(first, second)


def plain(inputs, gate_acts, out_grad, first_factor, second_factor):
    n = lax.axis_size("seq")
    width, extent = inputs.shape
    cols, rows = first_factor.shape[0], second_factor.shape[0]
    row_block, col_block = rows // n, cols // n
    grid = inputs.reshape(width, row_block, cols)
    first = first_factor.reshape(n, col_block, cols)
    second = second_factor.reshape(rows, n, row_block)

    def exchange(value):
        sent = lax.all_to_all(
            value.reshape(n, -1), "seq", split_axis=0, concat_axis=0, tiled=True
        )
        return sent.reshape(n, col_block, row_block, width)

    def einsum(spec, lhs, rhs):
        return jnp.einsum(spec, lhs, rhs, preferred_element_type=F32)

    received = exchange(einsum("cij,skj->skic", grid, first).astype(BF16))
    mixed = einsum("odgi,fog->idf", received, second)
    g = out_grad.reshape(width, col_block, rows).astype(F32)
    gate_grad = (g * mixed).astype(BF16).reshape(width, extent)
    mg = (g * gate_acts.reshape(width, col_block, rows).astype(F32)).astype(BF16)
    returned = exchange(einsum("vph,hox->opxv", mg, second).astype(BF16))
    second_term = einsum("wjq,ajtw->qat", mg, received).reshape(rows, rows)
    input_grad = einsum("skrc,skj->crj", returned, first).astype(BF16).reshape(width, extent)
    first_term = einsum("skrc,crj->skj", returned, grid).reshape(cols, cols)
    return input_grad, gate_grad, first_term, second_term


def local(inputs, gate_acts, out_grad, first_factor, second_factor):
    n = lax.axis_size("seq")
    width = inputs.shape[0]
    cols, rows = first_factor.shape[0], second_factor.shape[0]
    chans = lax.axis_size("chan")
    fits = (
        rows == cols
        and n % 2 == 0
        and width % (2 * LANES) == 0
        and rows % (n * PACK) == 0
        and LANES % (rows // n) == 0
        and rows % (n * chans * 8) == 0
        and chans > 1
        and n >= 4
    )
    args = (inputs, gate_acts, out_grad, first_factor, second_factor)
    if fits:
        input_grad, gate_grad, first_grad, second_grad = fused(*args)
        return *hand_out(input_grad, gate_grad), first_grad, second_grad
    input_grad, gate_grad, first_term, second_term = plain(*args)
    totals = lax.psum((first_term, second_term), "chan")
    first_grad = lax.psum_scatter(totals[0], "seq", scatter_dimension=0, tiled=True)
    second_grad = lax.psum_scatter(totals[1], "seq", scatter_dimension=0, tiled=True)
    return input_grad, gate_grad, first_grad, second_grad


def solution(mesh):
    return jax.shard_map(
        local,
        mesh=mesh,
        in_specs=(P("chan", "seq"), P("chan", "seq"), P("chan", "seq"), P(), P()),
        out_specs=(P("chan", "seq"), P("chan", "seq"), P("seq", None), P("seq", None)),
        check_vma=False,
    )
```

```python
import functools

import jax
import jax.numpy as jnp
from jax import lax
from jax.experimental import pallas as pl
from jax.experimental.pallas import tpu as pltpu
from jax.sharding import PartitionSpec as P

BF16 = jnp.bfloat16
F32 = jnp.float32
LANES = 128
PACK = 16


def dot_nn(lhs, rhs):
    return lax.dot_general(lhs, rhs, (((1,), (0,)), ((), ())), preferred_element_type=F32)


def dot_nt(lhs, rhs):
    return lax.dot_general(lhs, rhs, (((1,), (1,)), ((), ())), preferred_element_type=F32)


def dot_tn(lhs, rhs):
    return lax.dot_general(lhs, rhs, (((0,), (0,)), ((), ())), preferred_element_type=F32)


def group_bounds(count):
    return [0, count // 8, count // 2, count * 3 // 4, count]


def stream(count, loads, work, store=None):
    def body(step, carry):
        slot = lax.rem(step, 2)

        @pl.when(step + 1 < count)
        def _():
            for load in loads:
                load(step + 1, 1 - slot).start()

        for load in loads:
            load(step, slot).wait()
        if store is not None:

            @pl.when(step >= 2)
            def _():
                store(step - 2, slot).wait()

        work(step, slot)
        if store is not None:
            store(step, slot).start()
        return carry

    for load in loads:
        load(0, 0).start()
    lax.fori_loop(0, count, body, 0)
    if store is not None:
        for step in range(max(count - 2, 0), count):
            store(step, step % 2).wait()


def kernel(
    n, chans, low, x_hbm, q_hbm, g_hbm, a_ref, b_ref,
    dx_hbm, dq_hbm, d1_ref, d2_ref,
    out1, out2, got1, got2, turned, x_buf, g_buf, q_buf, y_buf, bt_ref, acc1, acc2,
    terms, land1, sums, land2, final, x_last,
    x_sem, g_sem, q_sem, y_sem, own_sem, send1, recv1, send2, recv2, send_sum, recv_sum, last_sem,
):
    me, my_chan = lax.axis_index("seq"), lax.axis_index("chan")
    width = x_hbm.shape[0]
    rows, cols = b_ref.shape[0], a_ref.shape[0]
    row_block, col_block = rows // n, cols // n
    bounds = group_bounds(row_block)
    lane_parts, halves = width // LANES, row_block // PACK

    def hop(d):
        return lax.rem(me + d, n)

    near, high = low * chans, n // low
    my_low, my_high = lax.rem(me, low), me // low
    my_near = my_low * chans + my_chan

    def near_device(d):
        slot = lax.rem(my_near + d, near)
        return slot, {"seq": my_high * low + slot // chans, "chan": lax.rem(slot, chans)}

    def remote(src, dst, kind, which, device):
        return pltpu.make_async_remote_copy(
            src_ref=src, dst_ref=dst,
            send_sem=send_sum.at[kind, which], recv_sem=recv_sum.at[kind, which],
            device_id=device, device_id_type=pl.DeviceIdType.MESH,
        )

    def await_sum(view, kind, which):
        pltpu.make_async_copy(view, view, recv_sum.at[kind, which]).wait()
        pltpu.make_async_copy(view, view, send_sum.at[kind, which]).wait()

    def sum_near_start(which):
        def body(d, carry):
            slot, device = near_device(d)
            remote(
                terms.at[which, slot], land1.at[which, my_near], 0, which, device
            ).start()
            return carry

        lax.fori_loop(1, near, body, 0)

    def sum_far_start(which):
        await_sum(land1.at[which, pl.ds(0, near - 1)], 0, which)
        sums[which] = terms[which, my_near]

        def add(d, carry):
            sums[which] += land1[which, lax.rem(my_near + d, near)]
            return carry

        lax.fori_loop(1, near, add, 0)

        def body(d, carry):
            to = lax.rem(my_high + d, high)
            remote(
                sums.at[which, to], land2.at[which, my_high], 1, which,
                {"seq": to * low + my_low, "chan": my_chan},
            ).start()
            return carry

        lax.fori_loop(1, high, body, 0)

    def sum_share_start(which):
        await_sum(land2.at[which, pl.ds(0, high - 1)], 1, which)
        final[which, my_chan] = sums[which, my_high]

        def add(d, carry):
            final[which, my_chan] += land2[which, lax.rem(my_high + d, high)]
            return carry

        lax.fori_loop(1, high, add, 0)

        def body(d, carry):
            remote(
                final.at[which, my_chan], final.at[which, my_chan], 2, which,
                {"seq": me, "chan": lax.rem(my_chan + d, chans)},
            ).start()
            return carry

        lax.fori_loop(1, chans, body, 0)

    def sum_end(which, out):
        await_sum(final.at[which, pl.ds(0, chans - 1)], 2, which)
        out[...] = final[which].reshape(out.shape)

    def put_terms(which, strip, value):
        share = row_block // chans
        for c in range(chans):
            terms[which, (strip % low) * chans + c, strip // low] = value[c * share:(c + 1) * share]

    barrier = pltpu.get_barrier_semaphore()

    def greet(d, carry):
        pl.semaphore_signal(
            barrier, inc=1, device_id={"seq": hop(d)}, device_id_type=pl.DeviceIdType.MESH
        )
        return carry

    lax.fori_loop(1, n, greet, 0)

    def greet_chan(d, carry):
        def body(spot, inner):
            pl.semaphore_signal(
                barrier, inc=1,
                device_id={"seq": my_high * low + spot, "chan": lax.rem(my_chan + d, chans)},
                device_id_type=pl.DeviceIdType.MESH,
            )
            return inner

        return lax.fori_loop(0, low, body, carry)

    lax.fori_loop(1, chans, greet_chan, 0)

    def load_x(step, slot):
        return pltpu.make_async_copy(
            x_hbm.at[:, pl.ds(pl.multiple_of(step * cols, LANES), cols)],
            x_buf.at[slot], x_sem.at[slot],
        )

    def load_g(step, slot):
        return pltpu.make_async_copy(
            g_hbm.at[:, pl.ds(pl.multiple_of(step * rows, LANES), rows)],
            g_buf.at[slot], g_sem.at[slot],
        )

    def load_q(step, slot):
        return pltpu.make_async_copy(
            q_hbm.at[:, pl.ds(pl.multiple_of(step * rows, LANES), rows)],
            q_buf.at[slot], q_sem.at[slot],
        )

    def send_first(group, peer):
        first, last = bounds[group], bounds[group + 1]
        return pltpu.make_async_remote_copy(
            src_ref=out1.at[peer, pl.ds(first, last - first)],
            dst_ref=got1.at[pl.ds(me * row_block + first, last - first)],
            send_sem=send1.at[group], recv_sem=recv1.at[group],
            device_id={"seq": peer}, device_id_type=pl.DeviceIdType.MESH,
        )

    def first_own():
        return pltpu.make_async_copy(
            out1.at[me], got1.at[pl.ds(me * row_block, row_block)], own_sem.at[0]
        )

    chunks = [(h, ch) for h in range(halves) for ch in range(lane_parts)]
    sends = [(h, pl.ds(0, lane_parts)) for h in range(halves - 1)]
    sends += [(halves - 1, pl.ds(ch, 1)) for ch in range(lane_parts)]

    def send_second(index, peer):
        h, lanes = sends[index]
        return pltpu.make_async_remote_copy(
            src_ref=out2.at[h, lanes, peer],
            dst_ref=got2.at[h, lanes, pl.ds(me * col_block, col_block)],
            send_sem=send2.at[index], recv_sem=recv2.at[index],
            device_id={"seq": peer}, device_id_type=pl.DeviceIdType.MESH,
        )

    def second_own():
        return pltpu.make_async_copy(
            out2.at[:, :, me],
            got2.at[:, :, pl.ds(me * col_block, col_block)], own_sem.at[1],
        )

    def to_all(send, index):
        def body(t, carry):
            d = (1 - lax.rem(t, 2)) * (n // 2) + (t + 1) // 2
            send(index, hop(d)).start()
            return carry

        lax.fori_loop(0, n - 1, body, 0)

    def await_first(group, sems):
        view = got1.at[pl.ds(0, (n - 1) * (bounds[group + 1] - bounds[group]))]
        pltpu.make_async_copy(view, view, sems.at[group]).wait()

    def await_second(index, sems):
        h, lanes = sends[index]
        view = got2.at[h, lanes, pl.ds(0, (n - 1) * col_block)]
        pltpu.make_async_copy(view, view, sems.at[index]).wait()

    for group, first in enumerate(bounds[:-1]):
        def inner_step(step, slot):
            value = dot_nt(a_ref[...], x_buf[slot]).astype(BF16)
            out1[:, first + step] = value.reshape(n, col_block, width)

        stream(bounds[group + 1] - first, [lambda s, slot: load_x(first + s, slot)], inner_step)
        if group == 0:
            pl.semaphore_wait(barrier, n - 1 + low * (chans - 1))
        to_all(send_first, group)
    first_own().start()

    for strip in range(rows // LANES):
        span = pl.ds(strip * LANES, LANES)
        bt_ref[span, :] = b_ref[:, span].T

    def back_step(step, slot):
        mg = (g_buf[slot].astype(F32) * q_buf[slot].astype(F32)).astype(BF16)
        value = dot_nt(bt_ref[...], mg).astype(BF16).reshape(n, halves, PACK, width)
        for h, ch in chunks:
            out2[h, ch, :, step] = value[:, h, :, ch * LANES:(ch + 1) * LANES]

    stream(col_block, [load_g, load_q], back_step)
    second_own().start()

    acc1[...] = jnp.zeros_like(acc1)
    acc2[...] = jnp.zeros_like(acc2)

    groups = len(bounds) - 1
    for group in range(groups - 1):
        await_first(group, recv1)
    to_all(send_second, 0)
    await_first(groups - 1, recv1)
    if len(sends) > 1:
        to_all(send_second, 1)
    first_own().wait()

    def turn(got, slot, total):
        def body(block, carry):
            value = got(pl.ds(pl.multiple_of(block * 8, 8), 8))
            turned[slot, pl.ds(pl.multiple_of(block * 8 * PACK, 8 * PACK), 8 * PACK), :] = (
                value.astype(F32).reshape(8 * PACK, LANES)
            )
            return carry

        lax.fori_loop(0, total // 8, body, 0)

    def pick(slot, step, total):
        return turned[slot, pl.ds(step, total, stride=PACK), :].astype(BF16)

    for h in range(col_block // PACK):
        for ch in range(lane_parts):
            lanes = pl.ds(ch * LANES, LANES)
            turn(lambda span: got1[span, pl.ds(h * PACK, PACK), lanes], ch, rows)

        def gate_step(step, slot):
            g = g_buf[slot].astype(F32)
            mg = (g * q_buf[slot].astype(F32)).astype(BF16)
            inner = jnp.concatenate([pick(ch, step, rows) for ch in range(lane_parts)], axis=1)
            y_buf[slot] = (g * dot_tn(inner, bt_ref[...])).astype(BF16)
            acc2[...] += dot_nn(inner, mg)

        def store_dq(step, slot):
            return pltpu.make_async_copy(
                y_buf.at[slot],
                dq_hbm.at[:, pl.ds(pl.multiple_of((h * PACK + step) * rows, LANES), rows)],
                y_sem.at[slot],
            )

        stream(
            PACK,
            [lambda s, slot: load_g(h * PACK + s, slot), lambda s, slot: load_q(h * PACK + s, slot)],
            gate_step, store_dq,
        )
        if h == 0:
            for index in range(2, len(sends)):
                to_all(send_second, index)

    for strip in range(rows // LANES):
        value = acc2[:, pl.ds(strip * LANES, LANES)].T
        for b in range(LANES // row_block):
            put_terms(1, strip * (LANES // row_block) + b, value[b * row_block:(b + 1) * row_block])
    sum_near_start(1)

    def last_x(index, step):
        h, ch = chunks[index]
        start = (h * PACK + step) * cols
        return pltpu.make_async_copy(
            x_hbm.at[pl.ds(ch * LANES, LANES), pl.ds(start, cols)],
            x_last.at[step // 2, pl.ds(step % 2 * LANES, LANES)], last_sem.at[step],
        )

    second_own().wait()
    for index, (h, ch) in enumerate(chunks):
        last = index == len(chunks) - 1
        if last:
            for step in range(PACK):
                last_x(index, step).start()
        if h == halves - 1 or ch == 0:
            await_second(h if h < halves - 1 else h + ch, recv2)
        turn(lambda span: got2[h, ch, span], 0, cols)
        span = pl.ds(ch * LANES, LANES)

        def block(ref, step):
            start = pl.multiple_of((h * PACK + step) * cols, LANES)
            return ref.at[span, pl.ds(start, cols)]

        def load_part(step, slot):
            return pltpu.make_async_copy(
                block(x_hbm, step), x_buf.at[slot, pl.ds(0, LANES)], x_sem.at[slot]
            )

        def store_part(step, slot):
            return pltpu.make_async_copy(
                y_buf.at[slot, pl.ds(0, LANES)], block(dx_hbm, step), y_sem.at[slot]
            )

        def term_step(step, slot):
            acc1[...] += dot_nn(pick(0, step, cols), x_buf[slot, pl.ds(0, LANES)])

        def pair_step(step, carry):
            both = jnp.concatenate(
                [pick(0, 2 * step, cols), pick(0, 2 * step + 1, cols)], axis=1
            )
            acc1[...] += dot_nn(both, x_last[step])
            return carry

        def input_step(step, slot):
            y_buf[slot, pl.ds(0, LANES)] = dot_tn(pick(0, step, cols), a_ref[...]).astype(BF16)

        def both_steps(step, slot):
            input_step(step, slot)
            term_step(step, slot)

        if not last:
            stream(PACK, [load_part], both_steps, store_part)
        else:
            for step in range(PACK):
                last_x(index, step).wait()
            lax.fori_loop(0, PACK // 2, pair_step, 0)
            for strip in range(n):
                put_terms(0, strip, acc1[pl.ds(strip * row_block, row_block), :])
            sum_near_start(0)
            stream(PACK, [], input_step, store_part)
        if index == 0:
            sum_far_start(1)
        if index == min(1, len(chunks) - 1):
            sum_share_start(1)

    sum_far_start(0)
    sum_share_start(0)
    sum_end(1, d2_ref)
    sum_end(0, d1_ref)

    for group in range(groups):
        await_first(group, send1)
    for index in range(len(sends)):
        await_second(index, send2)


def fused(inputs, gate_acts, out_grad, first_factor, second_factor):
    n = lax.axis_size("seq")
    width, extent = inputs.shape
    cols, rows = first_factor.shape[0], second_factor.shape[0]
    row_block, col_block = rows // n, cols // n
    chans = lax.axis_size("chan")
    low = max(d for d in range(1, n + 1) if n % d == 0 and d * d <= n)
    near, high, share = low * chans, n // low, row_block // chans
    halves, lane_parts = row_block // PACK, width // LANES
    groups, chunk_count = len(group_bounds(row_block)) - 1, halves - 1 + lane_parts
    vmem = pl.BlockSpec(memory_space=pltpu.VMEM)
    hbm = pl.BlockSpec(memory_space=pl.ANY)
    dma = pltpu.SemaphoreType.DMA
    long_side = max(rows, cols)
    flops = 12 * width * row_block * cols * rows
    return pl.pallas_call(
        functools.partial(kernel, n, chans, low),
        out_shape=(
            jax.ShapeDtypeStruct((width, extent), BF16),
            jax.ShapeDtypeStruct((width, extent), BF16),
            jax.ShapeDtypeStruct((cols // n, cols), F32),
            jax.ShapeDtypeStruct((rows // n, rows), F32),
        ),
        in_specs=[hbm, hbm, hbm, vmem, vmem],
        out_specs=(hbm, hbm, vmem, vmem),
        scratch_shapes=[
            pltpu.VMEM((n, row_block, col_block, width), BF16),
            pltpu.VMEM((halves, lane_parts, n, col_block, PACK, LANES), BF16),
            pltpu.VMEM((rows, col_block, width), BF16),
            pltpu.VMEM((halves, lane_parts, cols, PACK, LANES), BF16),
            pltpu.VMEM((width // LANES, long_side * PACK, LANES), F32),
            pltpu.VMEM((2, width, cols), BF16),
            pltpu.VMEM((2, width, rows), BF16),
            pltpu.VMEM((2, width, rows), BF16),
            pltpu.VMEM((2, width, long_side), BF16),
            pltpu.VMEM((rows, rows), BF16),
            pltpu.VMEM((cols, cols), F32),
            pltpu.VMEM((rows, rows), F32),
            pltpu.VMEM((2, near, high, share, long_side), F32),
            pltpu.VMEM((2, near, high, share, long_side), F32),
            pltpu.VMEM((2, high, share, long_side), F32),
            pltpu.VMEM((2, high, share, long_side), F32),
            pltpu.VMEM((2, chans, share, long_side), F32),
            pltpu.VMEM((PACK // 2, 2 * LANES, cols), BF16),
            dma((2,)), dma((2,)), dma((2,)), dma((2,)), dma((2,)),
            dma((groups,)), dma((groups,)), dma((chunk_count,)), dma((chunk_count,)),
            dma((3, 2)), dma((3, 2)), dma((PACK,)),
        ],
        compiler_params=pltpu.CompilerParams(
            collective_id=0, has_side_effects=True, vmem_limit_bytes=58 * 2**20
        ),
        cost_estimate=pl.CostEstimate(flops=flops, bytes_accessed=16 * width * extent, transcendentals=0),
    )(inputs, gate_acts, out_grad, first_factor, second_factor)


def copy_kernel(a_in, b_in, a_out, b_out):
    a_out[...] = a_in[...]
    b_out[...] = b_in[...]


def hand_out(first, second):
    rows = 2 * PACK
    spec = pl.BlockSpec((rows, first.shape[1]), lambda i: (i, 0))
    return pl.pallas_call(
        copy_kernel,
        out_shape=tuple(jax.ShapeDtypeStruct(v.shape, v.dtype) for v in (first, second)),
        grid=(first.shape[0] // rows,),
        in_specs=[spec, spec],
        out_specs=(spec, spec),
        compiler_params=pltpu.CompilerParams(vmem_limit_bytes=56 * 2**20),
        cost_estimate=pl.CostEstimate(flops=0, bytes_accessed=8 * first.size, transcendentals=0),
    )(first, second)


def plain(inputs, gate_acts, out_grad, first_factor, second_factor):
    n = lax.axis_size("seq")
    width, extent = inputs.shape
    cols, rows = first_factor.shape[0], second_factor.shape[0]
    row_block, col_block = rows // n, cols // n
    grid = inputs.reshape(width, row_block, cols)
    first = first_factor.reshape(n, col_block, cols)
    second = second_factor.reshape(rows, n, row_block)

    def exchange(value):
        sent = lax.all_to_all(
            value.reshape(n, -1), "seq", split_axis=0, concat_axis=0, tiled=True
        )
        return sent.reshape(n, col_block, row_block, width)

    def einsum(spec, lhs, rhs):
        return jnp.einsum(spec, lhs, rhs, preferred_element_type=F32)

    received = exchange(einsum("cij,skj->skic", grid, first).astype(BF16))
    mixed = einsum("odgi,fog->idf", received, second)
    g = out_grad.reshape(width, col_block, rows).astype(F32)
    gate_grad = (g * mixed).astype(BF16).reshape(width, extent)
    mg = (g * gate_acts.reshape(width, col_block, rows).astype(F32)).astype(BF16)
    returned = exchange(einsum("vph,hox->opxv", mg, second).astype(BF16))
    second_term = einsum("wjq,ajtw->qat", mg, received).reshape(rows, rows)
    input_grad = einsum("skrc,skj->crj", returned, first).astype(BF16).reshape(width, extent)
    first_term = einsum("skrc,crj->skj", returned, grid).reshape(cols, cols)
    return input_grad, gate_grad, first_term, second_term


def local(inputs, gate_acts, out_grad, first_factor, second_factor):
    n = lax.axis_size("seq")
    width = inputs.shape[0]
    cols, rows = first_factor.shape[0], second_factor.shape[0]
    chans = lax.axis_size("chan")
    fits = (
        rows == cols
        and n % 2 == 0
        and width % (2 * LANES) == 0
        and rows % (n * PACK) == 0
        and LANES % (rows // n) == 0
        and rows % (n * chans * 8) == 0
        and chans > 1
        and n >= 4
    )
    args = (inputs, gate_acts, out_grad, first_factor, second_factor)
    if fits:
        input_grad, gate_grad, first_grad, second_grad = fused(*args)
        return *hand_out(input_grad, gate_grad), first_grad, second_grad
    input_grad, gate_grad, first_term, second_term = plain(*args)
    totals = lax.psum((first_term, second_term), "chan")
    first_grad = lax.psum_scatter(totals[0], "seq", scatter_dimension=0, tiled=True)
    second_grad = lax.psum_scatter(totals[1], "seq", scatter_dimension=0, tiled=True)
    return input_grad, gate_grad, first_grad, second_grad


def solution(mesh):
    return jax.shard_map(
        local,
        mesh=mesh,
        in_specs=(P("chan", "seq"), P("chan", "seq"), P("chan", "seq"), P(), P()),
        out_specs=(P("chan", "seq"), P("chan", "seq"), P("seq", None), P("seq", None)),
        check_vma=False,
    )
```

```python
import functools

import jax
import jax.numpy as jnp
from jax import lax
from jax.experimental import pallas as pl
from jax.experimental.pallas import tpu as pltpu
from jax.sharding import PartitionSpec as P

BF16 = jnp.bfloat16
F32 = jnp.float32
LANES = 128
PACK = 16


def dot_nn(lhs, rhs):
    return lax.dot_general(lhs, rhs, (((1,), (0,)), ((), ())), preferred_element_type=F32)


def dot_nt(lhs, rhs):
    return lax.dot_general(lhs, rhs, (((1,), (1,)), ((), ())), preferred_element_type=F32)


def dot_tn(lhs, rhs):
    return lax.dot_general(lhs, rhs, (((0,), (0,)), ((), ())), preferred_element_type=F32)


def group_bounds(count):
    return [0, count // 8, count // 2, count * 3 // 4, count]


def stream(count, loads, work, store=None):
    def body(step, carry):
        slot = lax.rem(step, 2)

        @pl.when(step + 1 < count)
        def _():
            for load in loads:
                load(step + 1, 1 - slot).start()

        for load in loads:
            load(step, slot).wait()
        if store is not None:

            @pl.when(step >= 2)
            def _():
                store(step - 2, slot).wait()

        work(step, slot)
        if store is not None:
            store(step, slot).start()
        return carry

    for load in loads:
        load(0, 0).start()
    lax.fori_loop(0, count, body, 0)
    if store is not None:
        for step in range(max(count - 2, 0), count):
            store(step, step % 2).wait()


def kernel(
    n, chans, low, x_hbm, q_hbm, g_hbm, a_ref, b_ref,
    dx_hbm, dq_hbm, d1_ref, d2_ref,
    out1, out2, got1, got2, turned, x_buf, g_buf, q_buf, y_buf, bt_ref, acc1, acc2,
    terms, land1, sums, land2, whole, x_last,
    x_sem, g_sem, q_sem, y_sem, own_sem, send1, recv1, send2, recv2, send_sum, recv_sum, last_sem,
):
    me, my_chan = lax.axis_index("seq"), lax.axis_index("chan")
    width = x_hbm.shape[0]
    rows, cols = b_ref.shape[0], a_ref.shape[0]
    row_block, col_block = rows // n, cols // n
    bounds = group_bounds(row_block)
    lane_parts, halves = width // LANES, row_block // PACK

    def hop(d):
        return lax.rem(me + d, n)

    near, high = low * chans, n // low
    my_low, my_high = lax.rem(me, low), me // low
    my_near = my_low * chans + my_chan

    def near_device(d):
        slot = lax.rem(my_near + d, near)
        return slot, {"seq": my_high * low + slot // chans, "chan": lax.rem(slot, chans)}

    def remote(src, dst, kind, which, device):
        return pltpu.make_async_remote_copy(
            src_ref=src, dst_ref=dst,
            send_sem=send_sum.at[kind, which], recv_sem=recv_sum.at[kind, which],
            device_id=device, device_id_type=pl.DeviceIdType.MESH,
        )

    def await_sum(view, kind, which):
        pltpu.make_async_copy(view, view, recv_sum.at[kind, which]).wait()
        pltpu.make_async_copy(view, view, send_sum.at[kind, which]).wait()

    def sum_near_start(which, first, count):
        def body(d, carry):
            slot, device = near_device(d)
            span = pl.ds(first, count)
            remote(
                terms.at[which, slot, span], land1.at[which, my_near, span], 0, which, device
            ).start()
            return carry

        lax.fori_loop(1, near, body, 0)

    def sum_far_start(which):
        await_sum(land1.at[which, pl.ds(0, near - 1)], 0, which)
        sums[which] = terms[which, my_near]

        def add(d, carry):
            sums[which] += land1[which, lax.rem(my_near + d, near)]
            return carry

        lax.fori_loop(1, near, add, 0)

        land2[which, my_chan, my_high] = sums[which, my_high]

        def body(d, carry):
            spot = lax.rem(my_high * chans + my_chan + d, high * chans)
            to = spot // chans
            remote(
                sums.at[which, to], land2.at[which, my_chan, my_high], 1, which,
                {"seq": to * low + my_low, "chan": lax.rem(spot, chans)},
            ).start()
            return carry

        lax.fori_loop(1, high * chans, body, 0)

    def sum_end(which, out):
        share = row_block // chans
        view = whole.at[pl.ds(0, high * chans - 1)]
        await_sum(view, 1, which)
        for c in range(chans):
            total = land2[which, c, 0]
            for part in range(1, high):
                total += land2[which, c, part]
            out[pl.ds(c * share, share), :] = total

    def put_terms(which, strip, value):
        share = row_block // chans
        for c in range(chans):
            terms[which, (strip % low) * chans + c, strip // low] = value[c * share:(c + 1) * share]

    barrier = pltpu.get_barrier_semaphore()

    def greet(d, carry):
        spot = lax.rem(me * chans + my_chan + d, n * chans)
        pl.semaphore_signal(
            barrier, inc=1,
            device_id={"seq": spot // chans, "chan": lax.rem(spot, chans)},
            device_id_type=pl.DeviceIdType.MESH,
        )
        return carry

    lax.fori_loop(1, n * chans, greet, 0)

    def load_x(step, slot):
        return pltpu.make_async_copy(
            x_hbm.at[:, pl.ds(pl.multiple_of(step * cols, LANES), cols)],
            x_buf.at[slot], x_sem.at[slot],
        )

    def load_g(step, slot):
        return pltpu.make_async_copy(
            g_hbm.at[:, pl.ds(pl.multiple_of(step * rows, LANES), rows)],
            g_buf.at[slot], g_sem.at[slot],
        )

    def load_q(step, slot):
        return pltpu.make_async_copy(
            q_hbm.at[:, pl.ds(pl.multiple_of(step * rows, LANES), rows)],
            q_buf.at[slot], q_sem.at[slot],
        )

    def send_first(group, peer):
        first, last = bounds[group], bounds[group + 1]
        return pltpu.make_async_remote_copy(
            src_ref=out1.at[peer, pl.ds(first, last - first)],
            dst_ref=got1.at[pl.ds(me * row_block + first, last - first)],
            send_sem=send1.at[group], recv_sem=recv1.at[group],
            device_id={"seq": peer}, device_id_type=pl.DeviceIdType.MESH,
        )

    def first_own():
        return pltpu.make_async_copy(
            out1.at[me], got1.at[pl.ds(me * row_block, row_block)], own_sem.at[0]
        )

    chunks = [(h, ch) for h in range(halves) for ch in range(lane_parts)]
    sends = [(h, pl.ds(0, lane_parts)) for h in range(halves - 1)]
    sends += [(halves - 1, pl.ds(ch, 1)) for ch in range(lane_parts)]

    def send_second(index, peer):
        h, lanes = sends[index]
        return pltpu.make_async_remote_copy(
            src_ref=out2.at[h, lanes, peer],
            dst_ref=got2.at[h, lanes, pl.ds(me * col_block, col_block)],
            send_sem=send2.at[index], recv_sem=recv2.at[index],
            device_id={"seq": peer}, device_id_type=pl.DeviceIdType.MESH,
        )

    def second_own():
        return pltpu.make_async_copy(
            out2.at[:, :, me],
            got2.at[:, :, pl.ds(me * col_block, col_block)], own_sem.at[1],
        )

    def to_all(send, index):
        def body(t, carry):
            d = (1 - lax.rem(t, 2)) * (n // 2) + (t + 1) // 2
            send(index, hop(d)).start()
            return carry

        lax.fori_loop(0, n - 1, body, 0)

    def await_first(group, sems):
        view = got1.at[pl.ds(0, (n - 1) * (bounds[group + 1] - bounds[group]))]
        pltpu.make_async_copy(view, view, sems.at[group]).wait()

    def await_second(index, sems):
        h, lanes = sends[index]
        view = got2.at[h, lanes, pl.ds(0, (n - 1) * col_block)]
        pltpu.make_async_copy(view, view, sems.at[index]).wait()

    for group, first in enumerate(bounds[:-1]):
        def inner_step(step, slot):
            value = dot_nt(a_ref[...], x_buf[slot]).astype(BF16)
            out1[:, first + step] = value.reshape(n, col_block, width)

        stream(bounds[group + 1] - first, [lambda s, slot: load_x(first + s, slot)], inner_step)
        if group == 0:
            pl.semaphore_wait(barrier, n * chans - 1)
        to_all(send_first, group)
    first_own().start()

    for strip in range(rows // LANES):
        span = pl.ds(strip * LANES, LANES)
        bt_ref[span, :] = b_ref[:, span].T

    def back_step(step, slot):
        mg = (g_buf[slot].astype(F32) * q_buf[slot].astype(F32)).astype(BF16)
        value = dot_nt(bt_ref[...], mg).astype(BF16).reshape(n, halves, PACK, width)
        for h, ch in chunks:
            out2[h, ch, :, step] = value[:, h, :, ch * LANES:(ch + 1) * LANES]

    stream(col_block, [load_g, load_q], back_step)
    second_own().start()

    acc1[...] = jnp.zeros_like(acc1)
    acc2[...] = jnp.zeros_like(acc2)

    groups = len(bounds) - 1
    for group in range(groups - 1):
        await_first(group, recv1)
    to_all(send_second, 0)
    await_first(groups - 1, recv1)
    if len(sends) > 1:
        to_all(send_second, 1)
    first_own().wait()

    def turn(got, slot, total):
        def body(block, carry):
            value = got(pl.ds(pl.multiple_of(block * 8, 8), 8))
            turned[slot, pl.ds(pl.multiple_of(block * 8 * PACK, 8 * PACK), 8 * PACK), :] = (
                value.astype(F32).reshape(8 * PACK, LANES)
            )
            return carry

        lax.fori_loop(0, total // 8, body, 0)

    def pick(slot, step, total):
        return turned[slot, pl.ds(step, total, stride=PACK), :].astype(BF16)

    for h in range(col_block // PACK):
        for ch in range(lane_parts):
            lanes = pl.ds(ch * LANES, LANES)
            turn(lambda span: got1[span, pl.ds(h * PACK, PACK), lanes], ch, rows)

        def gate_step(step, slot):
            g = g_buf[slot].astype(F32)
            mg = (g * q_buf[slot].astype(F32)).astype(BF16)
            inner = jnp.concatenate([pick(ch, step, rows) for ch in range(lane_parts)], axis=1)
            y_buf[slot] = (g * dot_tn(inner, bt_ref[...])).astype(BF16)
            acc2[...] += dot_nn(inner, mg)

        def store_dq(step, slot):
            return pltpu.make_async_copy(
                y_buf.at[slot],
                dq_hbm.at[:, pl.ds(pl.multiple_of((h * PACK + step) * rows, LANES), rows)],
                y_sem.at[slot],
            )

        stream(
            PACK,
            [lambda s, slot: load_g(h * PACK + s, slot), lambda s, slot: load_q(h * PACK + s, slot)],
            gate_step, store_dq,
        )
        if h == 0:
            for index in range(2, len(sends)):
                to_all(send_second, index)

    for strip in range(rows // LANES):
        value = acc2[:, pl.ds(strip * LANES, LANES)].T
        for b in range(LANES // row_block):
            put_terms(1, strip * (LANES // row_block) + b, value[b * row_block:(b + 1) * row_block])
    sum_near_start(1, 0, high)

    def last_x(index, step):
        h, ch = chunks[index]
        start = (h * PACK + step) * cols
        return pltpu.make_async_copy(
            x_hbm.at[pl.ds(ch * LANES, LANES), pl.ds(start, cols)],
            x_last.at[step // 2, pl.ds(step % 2 * LANES, LANES)], last_sem.at[step],
        )

    second_own().wait()
    for index, (h, ch) in enumerate(chunks):
        last = index == len(chunks) - 1
        if last:
            for step in range(PACK):
                last_x(index, step).start()
        if h == halves - 1 or ch == 0:
            await_second(h if h < halves - 1 else h + ch, recv2)
        turn(lambda span: got2[h, ch, span], 0, cols)
        span = pl.ds(ch * LANES, LANES)

        def block(ref, step):
            start = pl.multiple_of((h * PACK + step) * cols, LANES)
            return ref.at[span, pl.ds(start, cols)]

        def load_part(step, slot):
            return pltpu.make_async_copy(
                block(x_hbm, step), x_buf.at[slot, pl.ds(0, LANES)], x_sem.at[slot]
            )

        def store_part(step, slot):
            return pltpu.make_async_copy(
                y_buf.at[slot, pl.ds(0, LANES)], block(dx_hbm, step), y_sem.at[slot]
            )

        def term_step(step, slot):
            acc1[...] += dot_nn(pick(0, step, cols), x_buf[slot, pl.ds(0, LANES)])

        def input_step(step, slot):
            y_buf[slot, pl.ds(0, LANES)] = dot_tn(pick(0, step, cols), a_ref[...]).astype(BF16)

        def both_steps(step, slot):
            input_step(step, slot)
            term_step(step, slot)

        if not last:
            stream(PACK, [load_part], both_steps, store_part)
        else:
            for step in range(PACK):
                last_x(index, step).wait()
            strips = 2 if high % 2 == 0 else 1
            tall = cols // strips
            for strip in range(strips):
                span_rows = pl.ds(strip * tall, tall)

                def pair_step(step, carry):
                    both = jnp.concatenate(
                        [
                            turned[
                                0, pl.ds(strip * tall * PACK + 2 * step + odd, tall, stride=PACK), :
                            ].astype(BF16)
                            for odd in range(2)
                        ],
                        axis=1,
                    )
                    acc1[span_rows, :] += dot_nn(both, x_last[step])
                    return carry

                lax.fori_loop(0, PACK // 2, pair_step, 0)
                owners = n // strips
                for owner in range(strip * owners, (strip + 1) * owners):
                    put_terms(0, owner, acc1[pl.ds(owner * row_block, row_block), :])
                sum_near_start(0, strip * (high // strips), high // strips)
            stream(PACK, [], input_step, store_part)
        if index == 0:
            sum_far_start(1)

    sum_far_start(0)
    sum_end(1, d2_ref)
    sum_end(0, d1_ref)

    for group in range(groups):
        await_first(group, send1)
    for index in range(len(sends)):
        await_second(index, send2)


def fused(inputs, gate_acts, out_grad, first_factor, second_factor):
    n = lax.axis_size("seq")
    width, extent = inputs.shape
    cols, rows = first_factor.shape[0], second_factor.shape[0]
    row_block, col_block = rows // n, cols // n
    chans = lax.axis_size("chan")
    low = max(d for d in range(1, n + 1) if n % d == 0 and d * d <= n)
    near, high, share = low * chans, n // low, row_block // chans
    halves, lane_parts = row_block // PACK, width // LANES
    groups, chunk_count = len(group_bounds(row_block)) - 1, halves - 1 + lane_parts
    vmem = pl.BlockSpec(memory_space=pltpu.VMEM)
    hbm = pl.BlockSpec(memory_space=pl.ANY)
    dma = pltpu.SemaphoreType.DMA
    long_side = max(rows, cols)
    flops = 12 * width * row_block * cols * rows
    return pl.pallas_call(
        functools.partial(kernel, n, chans, low),
        out_shape=(
            jax.ShapeDtypeStruct((width, extent), BF16),
            jax.ShapeDtypeStruct((width, extent), BF16),
            jax.ShapeDtypeStruct((cols // n, cols), F32),
            jax.ShapeDtypeStruct((rows // n, rows), F32),
        ),
        in_specs=[hbm, hbm, hbm, vmem, vmem],
        out_specs=(hbm, hbm, vmem, vmem),
        scratch_shapes=[
            pltpu.VMEM((n, row_block, col_block, width), BF16),
            pltpu.VMEM((halves, lane_parts, n, col_block, PACK, LANES), BF16),
            pltpu.VMEM((rows, col_block, width), BF16),
            pltpu.VMEM((halves, lane_parts, cols, PACK, LANES), BF16),
            pltpu.VMEM((width // LANES, long_side * PACK, LANES), F32),
            pltpu.VMEM((2, width, cols), BF16),
            pltpu.VMEM((2, width, rows), BF16),
            pltpu.VMEM((2, width, rows), BF16),
            pltpu.VMEM((2, width, long_side), BF16),
            pltpu.VMEM((rows, rows), BF16),
            pltpu.VMEM((cols, cols), F32),
            pltpu.VMEM((rows, rows), F32),
            pltpu.VMEM((2, near, high, share, long_side), F32),
            pltpu.VMEM((2, near, high, share, long_side), F32),
            pltpu.VMEM((2, high, share, long_side), F32),
            pltpu.VMEM((2, chans, high, share, long_side), F32),
            pltpu.VMEM((high * chans, share, long_side), F32),
            pltpu.VMEM((PACK // 2, 2 * LANES, cols), BF16),
            dma((2,)), dma((2,)), dma((2,)), dma((2,)), dma((2,)),
            dma((groups,)), dma((groups,)), dma((chunk_count,)), dma((chunk_count,)),
            dma((3, 2)), dma((3, 2)), dma((PACK,)),
        ],
        compiler_params=pltpu.CompilerParams(
            collective_id=0, has_side_effects=True, vmem_limit_bytes=58 * 2**20
        ),
        cost_estimate=pl.CostEstimate(flops=flops, bytes_accessed=16 * width * extent, transcendentals=0),
    )(inputs, gate_acts, out_grad, first_factor, second_factor)


def copy_kernel(a_in, b_in, a_out, b_out, held, in_sem, out_sem):
    pieces, rows = held.shape[1], held.shape[2]

    def move(which, piece, inward):
        span = pl.ds(piece * rows, rows)
        if inward:
            source = (a_in, b_in)[which].at[span]
            return pltpu.make_async_copy(source, held.at[which, piece], in_sem.at[which, piece])
        target = (a_out, b_out)[which].at[span]
        return pltpu.make_async_copy(held.at[which, piece], target, out_sem.at[which, piece])

    order = [(which, piece) for piece in range(pieces) for which in range(2)]
    for spot in order:
        move(*spot, True).start()
    for spot in order:
        move(*spot, True).wait()
        move(*spot, False).start()
    for spot in order:
        move(*spot, False).wait()


def hand_out(first, second):
    rows = 2 * PACK
    pieces = first.shape[0] // rows
    hbm = pl.BlockSpec(memory_space=pl.ANY)
    dma = pltpu.SemaphoreType.DMA
    return pl.pallas_call(
        copy_kernel,
        out_shape=tuple(jax.ShapeDtypeStruct(v.shape, v.dtype) for v in (first, second)),
        in_specs=[hbm, hbm],
        out_specs=(hbm, hbm),
        scratch_shapes=[
            pltpu.VMEM((2, pieces, rows, first.shape[1]), first.dtype),
            dma((2, pieces)), dma((2, pieces)),
        ],
        compiler_params=pltpu.CompilerParams(vmem_limit_bytes=56 * 2**20),
        cost_estimate=pl.CostEstimate(flops=0, bytes_accessed=8 * first.size, transcendentals=0),
    )(first, second)


def plain(inputs, gate_acts, out_grad, first_factor, second_factor):
    n = lax.axis_size("seq")
    width, extent = inputs.shape
    cols, rows = first_factor.shape[0], second_factor.shape[0]
    row_block, col_block = rows // n, cols // n
    grid = inputs.reshape(width, row_block, cols)
    first = first_factor.reshape(n, col_block, cols)
    second = second_factor.reshape(rows, n, row_block)

    def exchange(value):
        sent = lax.all_to_all(
            value.reshape(n, -1), "seq", split_axis=0, concat_axis=0, tiled=True
        )
        return sent.reshape(n, col_block, row_block, width)

    def einsum(spec, lhs, rhs):
        return jnp.einsum(spec, lhs, rhs, preferred_element_type=F32)

    received = exchange(einsum("cij,skj->skic", grid, first).astype(BF16))
    mixed = einsum("odgi,fog->idf", received, second)
    g = out_grad.reshape(width, col_block, rows).astype(F32)
    gate_grad = (g * mixed).astype(BF16).reshape(width, extent)
    mg = (g * gate_acts.reshape(width, col_block, rows).astype(F32)).astype(BF16)
    returned = exchange(einsum("vph,hox->opxv", mg, second).astype(BF16))
    second_term = einsum("wjq,ajtw->qat", mg, received).reshape(rows, rows)
    input_grad = einsum("skrc,skj->crj", returned, first).astype(BF16).reshape(width, extent)
    first_term = einsum("skrc,crj->skj", returned, grid).reshape(cols, cols)
    return input_grad, gate_grad, first_term, second_term


def local(inputs, gate_acts, out_grad, first_factor, second_factor):
    n = lax.axis_size("seq")
    width = inputs.shape[0]
    cols, rows = first_factor.shape[0], second_factor.shape[0]
    chans = lax.axis_size("chan")
    fits = (
        rows == cols
        and n % 2 == 0
        and width % (2 * LANES) == 0
        and rows % (n * PACK) == 0
        and LANES % (rows // n) == 0
        and rows % (n * chans * 8) == 0
        and chans > 1
        and n >= 4
    )
    args = (inputs, gate_acts, out_grad, first_factor, second_factor)
    if fits:
        input_grad, gate_grad, first_grad, second_grad = fused(*args)
        return *hand_out(input_grad, gate_grad), first_grad, second_grad
    input_grad, gate_grad, first_term, second_term = plain(*args)
    totals = lax.psum((first_term, second_term), "chan")
    first_grad = lax.psum_scatter(totals[0], "seq", scatter_dimension=0, tiled=True)
    second_grad = lax.psum_scatter(totals[1], "seq", scatter_dimension=0, tiled=True)
    return input_grad, gate_grad, first_grad, second_grad


def solution(mesh):
    return jax.shard_map(
        local,
        mesh=mesh,
        in_specs=(P("chan", "seq"), P("chan", "seq"), P("chan", "seq"), P(), P()),
        out_specs=(P("chan", "seq"), P("chan", "seq"), P("seq", None), P("seq", None)),
        check_vma=False,
    )
```
